32 devices in a mesh: groups: 2 (over y), row: 4 (over z), col: 2 (over x), chan: 2 (over core).
Axes of the slice: x: 2, y: 2, z: 4, core: 2. Of those that a mesh axis runs over, the one named last changes fastest.
Arguments:
- layer_input: bfloat16 [2, 64, 32, 512], P(None, None, ('groups', 'col'), 'row'), parts along dimension 2, may hold values from -6 to 6
- features: bfloat16 [2, 64, 32, 512], P(None, 'chan', ('groups', 'col'), 'row'), parts along dimension 2, may hold values from -6 to 6
- vol_target: bfloat16 [8, 40, 32, 512], P('chan', None, ('groups', 'col'), 'row'), parts along dimension 2, may hold values from -6 to 6
- offsets: int32 [4, 4], P('row', ('groups', 'col')), parts along dimension 1, may hold values from 0 to 2, as said below
- w_first: bfloat16 [64, 64, 3, 3], replicated, may hold values from -0.25 to 0.25
- w_second: bfloat16 [64, 64, 3, 3], replicated, may hold values from -0.25 to 0.25
Outputs:
- grad_features: bfloat16 [2, 64, 32, 512], P(None, 'chan', ('groups', 'col'), 'row'), parts along dimension 2
- grad_w_first: float32 [128, 64, 3, 3], P('groups'), parts along dimension 0
- grad_w_second: float32 [128, 64, 3, 3], P('groups'), parts along dimension 0
The draws below stay inside these ranges and needn't reach their ends.
There are 2 independent parts, one for each index of `groups`. The reference program is written for one: setup_inputs(seed, part) draws one part's arguments, and reference() takes and returns one part's arrays. A program takes and returns all parts, laid end to end along the dimension named above; an argument that names none is the same for every part. Nothing has to cross between parts.
Inputs may be any that keep to these rules, and one draw needn't show every extreme that they name: `offsets`: each tile's entry is at most its own tile row index along the epipolar direction; tiles of the first row have 0, and some tile has exactly 2.
All inputs are finite; a program needn't handle non-finite values.
Results may differ from the reference program's by a relative error of at most 0.005.
Values may be sent and summed in bfloat16 or wider, within the bound.
A program may use at most 64 MiB of HBM per device.

```python
import math
import jax
import jax.numpy as jnp
from jax import lax

CHANNELS = 64
GROUPS = 8
DISP = 40
MAXOFF = 2
BLOCK = 128
TILE_W = 8
NX = 16
NY = 512
TILES_Y = 4
TILES_X = 2


def draw_offsets(key, part):
    part_key = jax.random.fold_in(key, part)
    key_raw = jax.random.fold_in(part_key, 11)
    key_row = jax.random.fold_in(part_key, 12)
    key_col = jax.random.fold_in(part_key, 13)
    raw_values = jax.random.randint(key_raw, (TILES_Y, TILES_X), 0, MAXOFF + 1)
    tile_rows = lax.broadcasted_iota(jnp.int32, (TILES_Y, TILES_X), 0)
    tile_cols = lax.broadcasted_iota(jnp.int32, (TILES_Y, TILES_X), 1)
    bounded = jnp.minimum(raw_values, tile_rows)
    chosen_row = jax.random.randint(key_row, (), MAXOFF, TILES_Y)
    chosen_col = jax.random.randint(key_col, (), 0, TILES_X)
    picked = jnp.logical_and(tile_rows == chosen_row, tile_cols == chosen_col)
    return jnp.where(picked, MAXOFF, bounded).astype(jnp.int32)


def level_of(stream_key, dims, split, low, largest):
    loudness = 1.0
    for axis_at, blocks in split:
        draws = jax.random.uniform(jax.random.fold_in(jax.random.fold_in(stream_key, 6), axis_at), (blocks,), jnp.float32, low / len(split), largest / len(split))
        loudness = loudness * jnp.repeat(jnp.exp(draws), dims[axis_at] // blocks).reshape((-1,) + (1,) * (len(dims) - 1 - axis_at))
    return loudness


def centred(key, extent, spread, bound, shards=(), held_as=jnp.bfloat16):
    entries = spread * jax.random.normal(key, extent, jnp.float32)
    if shards:
        entries = entries * level_of(key, extent, shards, -0.22, 0.18)
    return jnp.clip(entries, -bound, bound).astype(held_as)


def setup_inputs(seed: int = 0, part: int = 0) -> dict:
    splits = jax.random.split(jax.random.key(seed), 7)
    part_keys = jax.random.split(jax.random.fold_in(splits[6], part), 7)
    return {
        "layer_input": centred(part_keys[0], (2, CHANNELS, NX, NY), 1.0, 6.0, ((2, 2), (3, 4))),
        "features": centred(part_keys[1], (2, CHANNELS, NX, NY), 1.0, 6.0, ((1, 2), (2, 2), (3, 4))),
        "vol_target": centred(part_keys[2], (GROUPS, DISP, NX, NY), 1.0, 6.0, ((0, 2), (2, 2), (3, 4))),
        "offsets": draw_offsets(jax.random.fold_in(jax.random.fold_in(splits[6], part), 71), part),
        "w_first": centred(splits[4], (CHANNELS, CHANNELS, 3, 3), (9 * CHANNELS) ** -0.5, 0.25),
        "w_second": centred(splits[5], (CHANNELS, CHANNELS, 3, 3), (9 * CHANNELS) ** -0.5, 0.25),
    }


def convolve(image, kernel):
    return lax.conv_general_dilated(image, kernel, (1, 1), 'SAME', precision=lax.Precision.HIGHEST)

def reference(layer_input, features, vol_target, offsets, w_first, w_second):
    group_size = CHANNELS // GROUPS
    input_f32 = layer_input.astype(jnp.float32)
    hidden = jnp.maximum(convolve(input_f32, w_first.astype(jnp.float32)), 0.0).astype(jnp.bfloat16)
    left_feat = features[0].astype(jnp.float32)
    right_feat = features[1].astype(jnp.float32)
    offset_map = jnp.repeat(jnp.repeat(offsets.T, TILE_W, axis=0), BLOCK, axis=1).astype(jnp.int32)
    padding = BLOCK * MAXOFF + DISP
    right_padded = jnp.pad(right_feat, ((0, 0), (0, 0), (padding, 0)))
    y_index = lax.broadcasted_iota(jnp.int32, (NX, NY), 1)
    columns = lax.broadcasted_iota(jnp.int32, (NX, NY), 0)

    def disparity_step(d, state_now):
        left_grad, right_grad = state_now
        source_rows = (y_index - d - BLOCK * offset_map + padding).astype(jnp.int32)
        shifted = right_padded[:, columns, source_rows]
        volume = (left_feat * shifted).reshape(GROUPS, group_size, NX, NY).sum(axis=1) / group_size
        target_plane = lax.dynamic_index_in_dim(vol_target, d, 1, keepdims=False).astype(jnp.float32)
        weighted = jnp.repeat(volume - target_plane, group_size, axis=0) / group_size
        left_grad = left_grad + weighted * shifted
        right_grad = right_grad.at[:, columns, source_rows].add(weighted * left_feat)
        return (left_grad, right_grad)
    initial = (jnp.zeros((CHANNELS, NX, NY), jnp.float32), jnp.zeros((CHANNELS, NX, NY + padding), jnp.float32))
    left_grad, right_grad = lax.fori_loop(0, DISP, disparity_step, initial)
    grad_features = jnp.stack([left_grad, right_grad[:, :, padding:]]).astype(jnp.bfloat16)
    grad_f32 = grad_features.astype(jnp.float32)
    _, pull_second = jax.vjp(convolve, hidden.astype(jnp.float32), w_second.astype(jnp.float32))
    hidden_pre, w2_sum = pull_second(grad_f32)
    hidden_grad = jnp.where(hidden > 0, hidden_pre, 0.0).astype(jnp.bfloat16)
    _, pull_first = jax.vjp(lambda kernel: convolve(input_f32, kernel), w_first.astype(jnp.float32))
    w1_sum, = pull_first(hidden_grad.astype(jnp.float32))
    factor = 1.0 / math.sqrt(2.0 * NX * NY)
    return (grad_features, w1_sum * factor, w2_sum * factor)
```

```python
import functools
import math

import jax
import jax.numpy as jnp
from jax import lax
from jax.experimental import pallas as pl
from jax.experimental.pallas import tpu as pltpu
from jax.sharding import PartitionSpec as P

MAXOFF = 2
REACH = MAXOFF + 1
MESH = pl.DeviceIdType.MESH
SIDES = [(dr, dc) for dr in (-1, 1) for dc in (-1, 0, 1)]
F32 = jnp.float32
BF16 = jnp.bfloat16


def vmem():
    return pl.BlockSpec(memory_space=pltpu.VMEM)


class Place:
    def __init__(self, sizes):
        self.sizes = sizes
        self.at = {axis: lax.axis_index(axis) for axis in sizes}

    def step(self, **moves):
        return {
            axis: lax.rem(self.at[axis] + (move + self.sizes[axis]), self.sizes[axis])
            for axis, move in moves.items()
        }


def greet(place, moves):
    barrier = pltpu.get_barrier_semaphore()
    for move in moves:
        back = {axis: -by for axis, by in move.items()}
        pl.semaphore_signal(barrier, inc=1, device_id=place.step(**back), device_id_type=MESH)
    pl.semaphore_wait(barrier, len(moves))


def send(place, move, src, dst, send_sem, recv_sem, at):
    copy = pltpu.make_async_remote_copy(
        src_ref=src,
        dst_ref=dst,
        send_sem=send_sem.at[at],
        recv_sem=recv_sem.at[at],
        device_id=place.step(**move),
        device_id_type=MESH,
    )
    copy.start()
    return copy


def packed_edges(tile_of, images, tile_w, lanes):
    width = lanes.shape[1]
    count = images * tile_w
    packed = jnp.zeros(lanes.shape, F32)
    for k in range(count):
        tile = tile_of(k // tile_w, k % tile_w)
        packed = jnp.where(lanes == k, pltpu.roll(tile, k + 1, 1), packed)
        packed = jnp.where(lanes == count + k, pltpu.roll(tile, count + k, 1), packed)
    return packed


def rolled(value, by):
    by = by % value.shape[-1]
    return value if by == 0 else pltpu.roll(value, by, value.ndim - 1)


def fill_views(views, place, tile_of, side_of, edges_of, images, tile_w, lanes):
    width = lanes.shape[1]
    count = images * tile_w
    row, col = place.at["row"], place.at["col"]
    rows, cols = place.sizes["row"], place.sizes["col"]
    inside_row = {-1: (row > 0).astype(F32), 1: (row < rows - 1).astype(F32)}
    inside_col = {-1: (col > 0).astype(F32), 0: 1.0, 1: (col < cols - 1).astype(F32)}
    for dc in (-1, 0, 1):
        before = edges_of(SIDES.index((-1, dc))) * (inside_row[-1] * inside_col[dc])
        after = edges_of(SIDES.index((1, dc))) * (inside_row[1] * inside_col[dc])
        places = {-1: [0], 0: range(1, tile_w + 1), 1: [tile_w + 1]}[dc]
        for n in range(images):
            for xx in places:
                if dc == 0:
                    tile = tile_of(n, xx - 1)
                    k = n * tile_w + xx - 1
                else:
                    tile = side_of(0 if dc < 0 else 1, n) * inside_col[dc]
                    k = n * tile_w + (tile_w - 1 if dc < 0 else 0)
                left = jnp.where(lanes == 0, rolled(before, -k), rolled(tile, 1))
                right = jnp.where(
                    lanes == width - 1, rolled(after, width - 1 - count - k), rolled(tile, -1)
                )
                views[n, xx, 0] = left.astype(BF16)
                views[n, xx, 1] = tile.astype(BF16)
                views[n, xx, 2] = right.astype(BF16)


def lane_index(shape):
    return lax.broadcasted_iota(jnp.int32, shape, len(shape) - 1)


def fetch_kernel(sizes, right_ref, image_ref, window_ref, edges_ref, side_ref, pack, send_sem, recv_sem):
    place = Place(sizes)
    images, tile_w, channels, width = image_ref.shape
    moves = [{"row": k} for k in range(1, REACH + 1)]
    moves += [{"col": 1}, {"col": -1}]
    moves += [{"row": -dr, "col": -dc} for dr, dc in SIDES]
    greet(place, moves)
    copies = []
    for k in range(REACH):
        copies.append(send(place, moves[k], right_ref, window_ref.at[k], send_sem, recv_sem, k))
    for side, x in ((0, tile_w - 1), (1, 0)):
        at = REACH + side
        copies.append(
            send(place, moves[at], image_ref.at[:, x], side_ref.at[side], send_sem, recv_sem, at)
        )
    lanes = lane_index((channels, width))
    pack[...] = packed_edges(
        lambda n, x: image_ref[n, x].astype(F32), images, tile_w, lanes
    ).astype(BF16)
    for j in range(len(SIDES)):
        at = REACH + 2 + j
        copies.append(send(place, moves[at], pack, edges_ref.at[j], send_sem, recv_sem, at))
    for copy in copies:
        copy.wait()


def correlate_kernel(
    sizes, offset_ref, left_ref, right_ref, window_ref, target_ref, image_ref, edges_ref, side_ref,
    w_ref, left_grad_ref, own_ref, out_ref, hidden_ref, views_ref, main_s, spill_s,
):
    place = Place(sizes)
    images, tile_w, channels, width = image_ref.shape
    groups, disp = target_ref.shape[:2]
    size = left_ref.shape[0] // groups
    inv = 1.0 / size
    offset = offset_ref[0, 0]
    row = place.at["row"]
    lanes = lane_index((tile_w, width))
    spill_in = [jnp.logical_and(offset + 1 == k, row >= k).astype(F32) for k in range(1, REACH + 1)]
    main_in = [(offset == k).astype(F32) for k in range(REACH)]

    def one_group(g, carry):
        first = pl.multiple_of(g * size, size)
        chans = pl.ds(first, size)
        got = [right_ref[chans].astype(F32)]
        got += [window_ref[k, chans].astype(F32) for k in range(REACH)]
        main_s[...] = sum(got[k] * main_in[k] for k in range(REACH))
        spill_s[...] = sum(got[k + 1] * spill_in[k] for k in range(REACH))

        def step(t, state):
            left_grad, main_grad, spill_grad = state
            left = left_ref[chans].astype(F32)
            for j in range(8):
                d = t * 8 + j
                keep = lanes < width - d
                shifted = pltpu.roll(jnp.where(keep, main_s[...], spill_s[...]), d, 2)
                volume = jnp.sum(left * shifted, axis=0) * inv
                weighted = (volume - target_ref[g, d].astype(F32)) * inv
                left_grad = left_grad + weighted * shifted
                back = pltpu.roll(weighted * left, lax.rem(width - d, width), 2)
                main_grad = main_grad + jnp.where(keep, back, 0.0)
                spill_grad = spill_grad + jnp.where(keep, 0.0, back)
            return left_grad, main_grad, spill_grad

        zero = jnp.zeros((size, tile_w, width), F32)
        left_grad, main_grad, spill_grad = lax.fori_loop(0, disp // 8, step, (zero, zero, zero))
        left_grad_ref[chans] = left_grad
        own_ref[chans] = main_grad * main_in[0]
        for k in range(1, REACH + 1):
            piece = spill_grad * spill_in[k - 1]
            if k < REACH:
                piece = piece + main_grad * main_in[k]
            out_ref[k - 1, chans] = piece.astype(BF16)
        return carry

    lax.fori_loop(0, groups, one_group, 0)
    fill_views(
        views_ref,
        place,
        lambda n, x: image_ref[n, x].astype(F32),
        lambda side, n: side_ref[side, n].astype(F32),
        lambda j: edges_ref[j].astype(F32),
        images,
        tile_w,
        lane_index((channels, width)),
    )
    for n in range(images):
        for x in range(tile_w):
            view = views_ref[n, x : x + 3].reshape(9 * channels, width)
            total = jnp.dot(w_ref[...], view, preferred_element_type=F32)
            hidden_ref[n, x] = jnp.maximum(total, 0.0).astype(BF16)


def gather_kernel(
    sizes, left_grad_ref, own_ref, out_ref, grad_ref, full_ref, edges_ref, side_ref,
    arrived, rounded, pack, send_sem, recv_sem,
):
    place = Place(sizes)
    local, tile_w, width = own_ref.shape
    images = 2
    chan = place.at["chan"]
    chans = sizes["chan"]
    back = [{"row": -k} for k in range(1, REACH + 1)]
    moves = []
    for dchan in range(1, chans):
        moves.append(("full", None, {"chan": dchan}))
    for dchan in range(chans):
        for side, dc in ((0, 1), (1, -1)):
            moves.append(("side", side, {"col": dc, "chan": dchan}))
    for dchan in range(chans):
        for j, (dr, dc) in enumerate(SIDES):
            moves.append(("edges", j, {"row": -dr, "col": -dc, "chan": dchan}))
    greet(place, back + [move for _, _, move in moves])
    copies = []
    for k in range(REACH):
        copies.append(send(place, back[k], out_ref.at[k], arrived.at[k], send_sem, recv_sem, k))
    left_grad = left_grad_ref[...].astype(BF16)
    grad_ref[0] = left_grad
    rounded[0] = left_grad.astype(F32)
    for x in range(tile_w):
        full_ref[chan, 0, x] = rounded[0, :, x, :].astype(BF16)
    for copy in copies:
        copy.wait()
    right_grad = own_ref[...]
    for k in range(REACH):
        right_grad = right_grad + arrived[k].astype(F32)
    right_grad = right_grad.astype(BF16)
    grad_ref[1] = right_grad
    rounded[1] = right_grad.astype(F32)
    for x in range(tile_w):
        full_ref[chan, 1, x] = rounded[1, :, x, :].astype(BF16)
    copies = []
    packed = False
    for at, (kind, index, move) in enumerate(moves, REACH):
        if kind == "full":
            src, dst = full_ref.at[chan], full_ref.at[chan]
        elif kind == "side":
            x = tile_w - 1 if index == 0 else 0
            src, dst = full_ref.at[chan, :, x], side_ref.at[index, :, chan]
        else:
            if not packed:
                pack[...] = packed_edges(
                    lambda n, x: rounded[n, :, x, :], images, tile_w, lane_index((local, width))
                ).astype(BF16)
                packed = True
            src, dst = pack, edges_ref.at[index, chan]
        copies.append(send(place, move, src, dst, send_sem, recv_sem, at))
    for copy in copies:
        copy.wait()


def weights_kernel(
    sizes, full_ref, edges_ref, side_ref, hidden_ref, input_views, w_ref, out_ref, views_ref
):
    place = Place(sizes)
    chans, images, tile_w, local, width = full_ref.shape
    channels = chans * local

    def joined(parts):
        return jnp.concatenate([p.astype(F32) for p in parts], axis=0)

    fill_views(
        views_ref,
        place,
        lambda n, x: joined([full_ref[c, n, x] for c in range(chans)]),
        lambda side, n: joined([side_ref[side, n, c] for c in range(chans)]),
        lambda j: joined([edges_ref[j, c] for c in range(chans)]),
        images,
        tile_w,
        lane_index((channels, width)),
    )
    contract = (((1,), (1,)), ((), ()))
    first = jnp.zeros((local, 9 * channels), F32)
    second = jnp.zeros((local, 9 * channels), F32)
    for n in range(images):
        for x in range(tile_w):
            view = views_ref[n, x : x + 3].reshape(9 * channels, width)
            hidden = hidden_ref[n, x]
            total = jnp.dot(w_ref[...], view, preferred_element_type=F32)
            hidden_grad = jnp.where(hidden.astype(F32) > 0, total, 0.0).astype(BF16)
            second += lax.dot_general(hidden, view, contract, preferred_element_type=F32)
            image = input_views[n, x : x + 3].reshape(9 * channels, width)
            first += lax.dot_general(hidden_grad, image, contract, preferred_element_type=F32)
    pixels = images * tile_w * sizes["col"] * width * sizes["row"]
    factor = 1.0 / math.sqrt(pixels)
    out_ref[:local] = first * factor
    out_ref[local:] = second * factor


def reduce_kernel(sizes, part_ref, out_ref, arrived, send_sem, recv_sem):
    place = Place(sizes)
    cols = sizes["col"]
    group = sizes["row"] * cols
    rows = part_ref.shape[0] // group
    chan = place.at["chan"]
    me = place.at["row"] * cols + place.at["col"]
    partner = {"chan": lax.rem(chan + 1, sizes["chan"])}

    def peer(by):
        rank = lax.rem(me + by + group, group)
        return rank, {"row": lax.div(rank, cols), "col": lax.rem(rank, cols)}

    def chunk(rank):
        return pl.ds(pl.multiple_of(rank * rows, rows), rows)

    barrier = pltpu.get_barrier_semaphore()
    for by in range(1, group):
        pl.semaphore_signal(barrier, inc=1, device_id=peer(-by)[1], device_id_type=MESH)
    pl.semaphore_signal(barrier, inc=1, device_id=partner, device_id_type=MESH)
    pl.semaphore_wait(barrier, group)

    def start(src, dst, at, device):
        copy = pltpu.make_async_remote_copy(
            src_ref=src, dst_ref=dst, send_sem=send_sem.at[at], recv_sem=recv_sem.at[at],
            device_id=device, device_id_type=MESH,
        )
        copy.start()
        return copy

    scattered = []
    for by in range(1, group):
        rank, device = peer(by)
        scattered.append(start(part_ref.at[chunk(rank)], arrived.at[by - 1], by - 1, device))
    total = part_ref[chunk(me)]
    for by in range(1, group):
        scattered[by - 1].wait()
        total = total + arrived[by - 1]
    out_ref[chan, chunk(me)] = total
    gathered = []
    mine = out_ref.at[chan, chunk(me)]
    for by in range(1, group):
        gathered.append(start(mine, mine, group - 1 + by - 1, peer(by)[1]))
    base = 2 * (group - 1)
    relayed = [start(mine, mine, base, partner)]
    for by in range(1, group):
        gathered[by - 1].wait()
        held = out_ref.at[chan, chunk(peer(-by)[0])]
        relayed.append(start(held, held, base + by, partner))
    for copy in relayed:
        copy.wait()


def body(sizes, layer_input, features, vol_target, offsets, w_first, w_second):
    images, channels, tile_w, width = layer_input.shape
    local = features.shape[1]
    chans = sizes["chan"]
    shape = jax.ShapeDtypeStruct
    dma = pltpu.SemaphoreType.DMA
    first_ch = lax.axis_index("chan") * local
    limit = 48 * 1024 * 1024

    def call(kernel, out_shape, scratch, operands, collective_id=None, specs=None):
        params = {"vmem_limit_bytes": limit}
        if collective_id is not None:
            params.update(collective_id=collective_id, has_side_effects=True)
        return pl.pallas_call(
            functools.partial(kernel, sizes),
            out_shape=out_shape,
            in_specs=specs or [vmem()] * len(operands),
            out_specs=jax.tree.map(lambda _: vmem(), out_shape),
            scratch_shapes=scratch,
            compiler_params=pltpu.CompilerParams(**params),
        )(*operands)

    image = layer_input.transpose(0, 2, 1, 3)
    w1 = lax.dynamic_slice_in_dim(w_first, first_ch, local, 0)
    w1 = w1.transpose(0, 2, 3, 1).reshape(local, 9 * channels)
    w2 = lax.dynamic_slice_in_dim(w_second, first_ch, local, 1)
    w2 = w2[:, :, ::-1, ::-1].transpose(1, 2, 3, 0).reshape(local, 9 * channels)

    count = REACH + 2 + len(SIDES)
    window, edges, side = call(
        fetch_kernel,
        [
            shape((REACH, local, tile_w, width), BF16),
            shape((len(SIDES), channels, width), BF16),
            shape((2, images, channels, width), BF16),
        ],
        [pltpu.VMEM((channels, width), BF16), dma((count,)), dma((count,))],
        (features[1], image),
        0,
    )
    views_shape = (images, tile_w + 2, 3, channels, width)
    size = local // vol_target.shape[0]
    left_grad, own, outgoing, hidden, input_views = call(
        correlate_kernel,
        [
            shape((local, tile_w, width), F32),
            shape((local, tile_w, width), F32),
            shape((REACH, local, tile_w, width), BF16),
            shape((images, tile_w, local, width), BF16),
            shape(views_shape, BF16),
        ],
        [pltpu.VMEM((size, tile_w, width), F32)] * 2,
        (offsets, features[0], features[1], window, vol_target, image, edges, side, w1),
        specs=[pl.BlockSpec(memory_space=pltpu.SMEM)] + [vmem()] * 8,
    )
    count = REACH + (chans - 1) + chans * (2 + len(SIDES))
    grad_features, full, grad_edges, grad_side = call(
        gather_kernel,
        [
            shape((2, local, tile_w, width), BF16),
            shape((chans, 2, tile_w, local, width), BF16),
            shape((len(SIDES), chans, local, width), BF16),
            shape((2, 2, chans, local, width), BF16),
        ],
        [
            pltpu.VMEM((REACH, local, tile_w, width), BF16),
            pltpu.VMEM((2, local, tile_w, width), F32),
            pltpu.VMEM((local, width), BF16),
            dma((count,)),
            dma((count,)),
        ],
        (left_grad, own, outgoing),
        1,
    )
    partial = call(
        weights_kernel,
        shape((2 * local, 9 * channels), F32),
        [pltpu.VMEM(views_shape, BF16)],
        (full, grad_edges, grad_side, hidden, input_views, w2),
    )
    group = sizes["row"] * sizes["col"]
    if chans == 2 and (2 * local) % (8 * group) == 0:
        rows = 2 * local // group
        count = 2 * (group - 1) + group
        summed = call(
            reduce_kernel,
            shape((chans, 2 * local, 9 * channels), F32),
            [pltpu.VMEM((group - 1, rows, 9 * channels), F32), dma((count,)), dma((count,))],
            (partial,),
            2,
        )
    else:
        summed = lax.all_gather(lax.psum(partial, ("row", "col")), "chan")
    first = summed[:, :local].reshape(channels, 3, 3, channels).transpose(0, 3, 1, 2)
    second = summed[:, local:].reshape(channels, 3, 3, channels)[:, ::-1, ::-1]
    return grad_features, first, second.transpose(3, 0, 1, 2)


def solution(mesh):
    return jax.shard_map(
        functools.partial(body, dict(mesh.shape)),
        mesh=mesh,
        in_specs=(
            P(None, None, ("groups", "col"), "row"),
            P(None, "chan", ("groups", "col"), "row"),
            P("chan", None, ("groups", "col"), "row"),
            P("row", ("groups", "col")),
            P(),
            P(),
        ),
        out_specs=(
            P(None, "chan", ("groups", "col"), "row"),
            P("groups", None, None, None),
            P("groups", None, None, None),
        ),
        check_vma=False,
    )
```

```python
import functools
import math

import jax
import jax.numpy as jnp
from jax import lax
from jax.experimental import pallas as pl
from jax.experimental.pallas import tpu as pltpu
from jax.sharding import PartitionSpec as P

MAXOFF = 2
REACH = MAXOFF + 1
MESH = pl.DeviceIdType.MESH
SIDES = [(dr, dc) for dr in (-1, 1) for dc in (-1, 0, 1)]
F32 = jnp.float32
BF16 = jnp.bfloat16


def vmem():
    return pl.BlockSpec(memory_space=pltpu.VMEM)


def rolled(value, by):
    by = by % value.shape[-1]
    return value if by == 0 else pltpu.roll(value, by, value.ndim - 1)


def lane_index(shape):
    return lax.broadcasted_iota(jnp.int32, shape, len(shape) - 1)


def either(condition, value, lanes):
    start = jnp.where(condition, 0, lanes.shape[-1])
    return jnp.where(lanes >= start, value, 0.0)


class Links:
    def __init__(self, sizes, send_sem, recv_sem):
        self.sizes = sizes
        self.at = {axis: lax.axis_index(axis) for axis in sizes}
        self.send_sem, self.recv_sem = send_sem, recv_sem
        self.used = 0

    def exists(self, move):
        found = None
        for axis, by in move.items():
            if axis == "chan" or by == 0:
                continue
            there = self.at[axis] + by
            here = jnp.logical_and(there >= 0, there < self.sizes[axis])
            found = here if found is None else jnp.logical_and(found, here)
        return found

    def where(self, move):
        return {
            axis: lax.rem(self.at[axis] + (by + self.sizes[axis]), self.sizes[axis])
            for axis, by in move.items()
        }

    def when(self, move, action):
        found = self.exists(move)
        if found is None:
            action()
        else:
            pl.when(found)(action)

    def back(self, move):
        return {axis: -by for axis, by in move.items()}

    def greet(self, moves, group):
        barrier = pltpu.get_barrier_semaphore()
        count = 0
        for move in moves:
            origin = self.back(move)
            self.when(
                origin,
                lambda origin=origin: pl.semaphore_signal(
                    barrier, inc=1, device_id=self.where(origin), device_id_type=MESH
                ),
            )
            found = self.exists(move)
            count = count + (1 if found is None else found.astype(jnp.int32))
        for by in range(1, group):
            device = self.peer(-by, group)[1]
            pl.semaphore_signal(barrier, inc=1, device_id=device, device_id_type=MESH)
            count = count + 1
        pl.semaphore_wait(barrier, count)

    def peer(self, by, group):
        cols = self.sizes["col"]
        me = self.at["row"] * cols + self.at["col"]
        rank = lax.rem(me + by + group, group)
        return rank, {"row": lax.div(rank, cols), "col": lax.rem(rank, cols)}

    def copy(self, src, dst, device):
        at = self.used
        self.used += 1
        return pltpu.make_async_remote_copy(
            src_ref=src,
            dst_ref=dst,
            send_sem=self.send_sem.at[at],
            recv_sem=self.recv_sem.at[at],
            device_id=device,
            device_id_type=MESH,
        )

    def send(self, move, src, dst):
        copy = self.copy(src, dst, self.where(move))
        self.when(move, copy.start)
        return move, copy

    def received(self, sent):
        for move, copy in sent:
            self.when(self.back(move), copy.wait_recv)

    def left(self, sent):
        for move, copy in sent:
            self.when(move, copy.wait_send)


def packed_edges(tiles, lanes):
    packed = jnp.zeros(lanes.shape, F32)
    for k, tile in enumerate(tiles):
        packed = jnp.where(lanes == k, rolled(tile, k + 1), packed)
        packed = jnp.where(lanes == len(tiles) + k, rolled(tile, len(tiles) + k), packed)
    return packed


def fill_views(views, links, n, tile_of, side_of, edges_of, tile_w, lanes):
    width = lanes.shape[1]
    for dc in (-1, 0, 1):
        before = either(
            links.exists({"row": -1, "col": dc}), edges_of(SIDES.index((-1, dc))), lanes
        )
        after = either(links.exists({"row": 1, "col": dc}), edges_of(SIDES.index((1, dc))), lanes)
        for xx in {-1: [0], 0: range(1, tile_w + 1), 1: [tile_w + 1]}[dc]:
            if dc == 0:
                tile, k = tile_of(xx - 1), xx - 1
            else:
                tile = either(links.exists({"col": dc}), side_of(0 if dc < 0 else 1), lanes)
                k = tile_w - 1 if dc < 0 else 0
            left = jnp.where(lanes == 0, rolled(before, -k), rolled(tile, 1))
            right = jnp.where(
                lanes == width - 1, rolled(after, width - 1 - tile_w - k), rolled(tile, -1)
            )
            views[n, xx, 0] = left.astype(BF16)
            views[n, xx, 1] = tile.astype(BF16)
            views[n, xx, 2] = right.astype(BF16)


EDGE_MOVES = [{"row": -dr, "col": -dc} for dr, dc in SIDES]
SIDE_MOVES = [{"col": 1}, {"col": -1}]


def whole_kernel(
    sizes, group, offset_ref, features_ref, target_ref, image_ref, w1_ref, w2_ref,
    grad_ref, sum_ref,
    image, image_pack, image_edges, image_side, image_views, hidden_s, w1, w2, turned, turned_w,
    window, main_s, spill_s, outgoing, arrived, own, rounded, full, grad_pack, grad_edges,
    grad_side, grad_views, part, parts, send_sem, recv_sem,
):
    links = Links(sizes, send_sem, recv_sem)
    images, channels, tile_w, width = image_ref.shape
    local = features_ref.shape[1]
    groups, disp = target_ref.shape[:2]
    size = local // groups
    inv = 1.0 / size
    chans = sizes["chan"]
    chan = links.at["chan"]
    row = links.at["row"]
    direct = group > 0
    forward = [{"row": k} for k in range(1, REACH + 1)]
    backward = [{"row": -k} for k in range(1, REACH + 1)]
    with_chan = [{**move, "chan": c} for move in EDGE_MOVES + SIDE_MOVES for c in range(chans)]
    partners = [{"chan": c} for c in range(1, chans)]
    links.greet(forward + backward + with_chan + partners, group)
    pending = []

    def parts_of(g):
        return pl.ds(g * size, size)

    fetched = []
    for g in range(groups):
        fetched.append([
            links.send(
                forward[k], features_ref.at[1, parts_of(g)], window.at[k, parts_of(g)]
            )
            for k in range(REACH)
        ])
        pending += fetched[-1]

    lanes = lane_index((channels, width))
    for n in range(images):
        turned[...] = image_ref[n].astype(F32)
        for x in range(tile_w):
            image[n, x] = turned[:, x, :].astype(BF16)
    border = [
        links.send(move, image.at[:, x], image_side.at[side])
        for side, (x, move) in enumerate(zip((tile_w - 1, 0), SIDE_MOVES))
    ]
    for n in range(images):
        image_pack[n] = packed_edges(
            [image[n, x].astype(F32) for x in range(tile_w)], lanes
        ).astype(BF16)
    border += [
        links.send(move, image_pack, image_edges.at[j]) for j, move in enumerate(EDGE_MOVES)
    ]
    pending += border

    first_ch = pl.multiple_of(chan * local, local)
    mine = pl.ds(first_ch, local)
    taps = [(a, b) for a in range(3) for b in range(3)]
    w1[...] = jnp.concatenate([w1_ref[a, b, mine].astype(F32) for a, b in taps], axis=1).astype(BF16)
    flipped = jnp.concatenate([w2_ref[2 - a, 2 - b].astype(F32) for a, b in taps], axis=0)
    turned_w[...] = flipped.T
    w2[...] = turned_w[mine].astype(BF16)

    links.received(border)
    for n in range(images):
        fill_views(
            image_views, links, n,
            lambda x, n=n: image[n, x].astype(F32),
            lambda side, n=n: image_side[side, n].astype(F32),
            lambda j, n=n: image_edges[j, n].astype(F32),
            tile_w, lanes,
        )
    for n in range(images):
        for x in range(tile_w):
            view = image_views[n, x : x + 3].reshape(9 * channels, width)
            total = jnp.dot(w1[...], view, preferred_element_type=F32)
            hidden_s[n, x] = jnp.maximum(total, 0.0).astype(BF16)

    small = lane_index((tile_w, width))
    offset = jnp.broadcast_to(offset_ref[...], (tile_w, width))
    inside = small * 0 + row
    main_in = [offset == k for k in range(REACH)]
    spill_in = [
        jnp.logical_and(offset + 1 == k, inside >= k) for k in range(1, REACH + 1)
    ]
    returned = []
    for g in range(groups):
        links.received(fetched[g])
        chosen = parts_of(g)
        main = jnp.where(main_in[0], features_ref[1, chosen].astype(F32), 0.0)
        spill = jnp.zeros_like(main)
        for k in range(REACH):
            got = window[k, chosen].astype(F32)
            spill = jnp.where(spill_in[k], got, spill)
            if k + 1 < REACH:
                main = jnp.where(main_in[k + 1], got, main)
        main_s[...] = main
        spill_s[...] = spill

        def step(t, state, g=g, chosen=chosen):
            left_grad, main_grad, spill_grad = state
            left = features_ref[0, chosen].astype(F32)
            for j in range(8):
                d = t * 8 + j
                keep = small < width - d
                shifted = pltpu.roll(jnp.where(keep, main_s[...], spill_s[...]), d, 2)
                volume = jnp.sum(left * shifted, axis=0) * inv
                weighted = (volume - target_ref[g, d].astype(F32)) * inv
                left_grad = left_grad + weighted * shifted
                back = pltpu.roll(weighted * left, lax.rem(width - d, width), 2)
                main_grad = main_grad + jnp.where(keep, back, 0.0)
                spill_grad = spill_grad + jnp.where(keep, 0.0, back)
            return left_grad, main_grad, spill_grad

        zero = jnp.zeros((size, tile_w, width), F32)
        left_grad, main_grad, spill_grad = lax.fori_loop(0, disp // 8, step, (zero, zero, zero))
        for k in range(1, REACH + 1):
            piece = jnp.where(spill_in[k - 1], spill_grad, 0.0)
            if k < REACH:
                piece = jnp.where(main_in[k], main_grad, piece)
            outgoing[k - 1, chosen] = piece.astype(BF16)
        returned.append([
            links.send(backward[k], outgoing.at[k, chosen], arrived.at[k, chosen])
            for k in range(REACH)
        ])
        pending += returned[-1]
        own[chosen] = jnp.where(main_in[0], main_grad, 0.0)
        left_grad = left_grad.astype(BF16)
        grad_ref[0, chosen] = left_grad
        rounded[0, chosen] = left_grad.astype(F32)

    slim = lane_index((local, width))

    def share(n):
        for x in range(tile_w):
            full[n, chan, x] = rounded[n, :, x, :].astype(BF16)
        sent = [links.send(move, full.at[n, chan], full.at[n, chan]) for move in partners]
        for c in range(chans):
            for side, (x, move) in enumerate(zip((tile_w - 1, 0), SIDE_MOVES)):
                sent.append(links.send(
                    {**move, "chan": c}, full.at[n, chan, x], grad_side.at[n, side, chan]
                ))
        grad_pack[n] = packed_edges(
            [rounded[n, :, x, :] for x in range(tile_w)], slim
        ).astype(BF16)
        for c in range(chans):
            for j, move in enumerate(EDGE_MOVES):
                sent.append(links.send(
                    {**move, "chan": c}, grad_pack.at[n], grad_edges.at[n, j, chan]
                ))
        return sent

    def joined(pieces):
        return jnp.concatenate([p.astype(F32) for p in pieces], axis=0)

    contract = (((1,), (1,)), ((), ()))

    def gradients(n, first, second):
        fill_views(
            grad_views, links, n,
            lambda x: joined([full[n, c, x] for c in range(chans)]),
            lambda side: joined([grad_side[n, side, c] for c in range(chans)]),
            lambda j: joined([grad_edges[n, j, c] for c in range(chans)]),
            tile_w, lanes,
        )
        for x in range(tile_w):
            view = grad_views[n, x : x + 3].reshape(9 * channels, width)
            hidden = hidden_s[n, x]
            total = jnp.dot(w2[...], view, preferred_element_type=F32)
            hidden_grad = jnp.where(hidden.astype(F32) > 0, total, 0.0).astype(BF16)
            second += lax.dot_general(hidden, view, contract, preferred_element_type=F32)
            seen = image_views[n, x : x + 3].reshape(9 * channels, width)
            first += lax.dot_general(hidden_grad, seen, contract, preferred_element_type=F32)
        return first, second

    left_sent = share(0)
    for g in range(groups):
        links.received(returned[g])
        chosen = parts_of(g)
        right_grad = own[chosen]
        for k in range(REACH):
            there = inside + (k + 1) < sizes["row"]
            right_grad = right_grad + jnp.where(there, arrived[k, chosen].astype(F32), 0.0)
        right_grad = right_grad.astype(BF16)
        grad_ref[1, chosen] = right_grad
        rounded[1, chosen] = right_grad.astype(F32)
    right_sent = share(1)
    pending += left_sent + right_sent
    empty = jnp.zeros((local, 9 * channels), F32)
    links.received(left_sent)
    first, second = gradients(0, empty, empty)
    links.received(right_sent)
    first, second = gradients(1, first, second)
    pixels = images * tile_w * sizes["col"] * width * sizes["row"]
    factor = 1.0 / math.sqrt(pixels)
    first, second = first * factor, second * factor

    if direct:
        rows = 2 * local // group
        half = group // 2
        for j in range(half):
            part[j] = first[j * rows : (j + 1) * rows].astype(BF16)
            part[half + j] = second[j * rows : (j + 1) * rows].astype(BF16)
        scattered, gathered, relayed = [], [], []
        for by in range(1, group):
            rank, device = links.peer(by, group)
            scattered.append(links.copy(part.at[rank], parts.at[by - 1], device))
            scattered[-1].start()
        me = links.peer(0, group)[0]
        total = part[me].astype(F32)
        for by in range(1, group):
            scattered[by - 1].wait_recv()
            total = total + parts[by - 1].astype(F32)
        sum_ref[chan, me] = total.astype(BF16)
        partner = links.where(partners[0])
        held = sum_ref.at[chan, me]
        for by in range(1, group):
            gathered.append(links.copy(held, held, links.peer(by, group)[1]))
            gathered[-1].start()
        relayed.append(links.copy(held, held, partner))
        relayed[-1].start()
        for by in range(1, group):
            gathered[by - 1].wait_recv()
            held = sum_ref.at[chan, links.peer(-by, group)[0]]
            relayed.append(links.copy(held, held, partner))
            relayed[-1].start()
        for copy in relayed:
            copy.wait_recv()
        for copy in scattered + gathered + relayed:
            copy.wait_send()
    else:
        sum_ref[:local] = first
        sum_ref[local:] = second
    links.left(pending)


def write_kernel(sum_ref, first_ref, second_ref):
    chans, pieces = sum_ref.shape[:2]
    channels = first_ref.shape[1]
    half = pieces // 2

    def rows(pick):
        return jnp.concatenate(
            [sum_ref[c, j].astype(F32) for c in range(chans) for j in pick], axis=0
        )

    first = rows(range(half))
    second = rows(range(half, pieces)).T
    for t in range(9):
        chosen = slice(t * channels, (t + 1) * channels)
        first_ref[t] = first[:, chosen]
        second_ref[8 - t] = second[chosen]


def body(sizes, layer_input, features, vol_target, offsets, w_first, w_second):
    images, channels, tile_w, width = layer_input.shape
    local = features.shape[1]
    chans = sizes["chan"]
    shape = jax.ShapeDtypeStruct
    dma = pltpu.SemaphoreType.DMA
    scratch = pltpu.VMEM
    size = local // vol_target.shape[0]
    group = sizes["row"] * sizes["col"]
    if chans != 2 or group % 2 or (2 * local) % (8 * group):
        group = 0
    rows = 2 * local // max(group, 2)
    views = (images, tile_w + 2, 3, channels, width)
    tile = (local, tile_w, width)
    edge = (len(SIDES), images, channels, width)
    count = 2 * REACH * vol_target.shape[0] + 2 + len(SIDES)
    count += images * ((chans - 1) + chans * (2 + len(SIDES))) + 3 * group
    if group:
        summed_shape = shape((chans, group, rows, 9 * channels), BF16)
    else:
        summed_shape = shape((2 * local, 9 * channels), F32)
    grad_features, summed = pl.pallas_call(
        functools.partial(whole_kernel, sizes, group),
        out_shape=[shape((2,) + tile, BF16), summed_shape],
        in_specs=[vmem()] * 6,
        out_specs=[vmem()] * 2,
        scratch_shapes=[
            scratch((images, tile_w, channels, width), BF16),
            scratch((images, channels, width), BF16),
            scratch(edge, BF16),
            scratch((2, images, channels, width), BF16),
            scratch(views, BF16),
            scratch((images, tile_w, local, width), BF16),
            scratch((local, 9 * channels), BF16),
            scratch((local, 9 * channels), BF16),
            scratch((channels, tile_w, width), F32),
            scratch((channels, 9 * channels), F32),
            scratch((REACH,) + tile, BF16),
            scratch((size, tile_w, width), F32),
            scratch((size, tile_w, width), F32),
            scratch((REACH,) + tile, BF16),
            scratch((REACH,) + tile, BF16),
            scratch(tile, F32),
            scratch((2,) + tile, F32),
            scratch((2, chans, tile_w, local, width), BF16),
            scratch((2, local, width), BF16),
            scratch((2, len(SIDES), chans, local, width), BF16),
            scratch((2, 2, chans, local, width), BF16),
            scratch(views, BF16),
            scratch((max(group, 2), rows, 9 * channels), BF16),
            scratch((max(group, 2), rows, 9 * channels), BF16),
            dma((count,)),
            dma((count,)),
        ],
        compiler_params=pltpu.CompilerParams(
            collective_id=0, has_side_effects=True, vmem_limit_bytes=48 * 1024 * 1024
        ),
    )(
        offsets,
        features,
        vol_target,
        layer_input,
        w_first.transpose(2, 3, 0, 1),
        w_second.transpose(2, 3, 0, 1),
    )
    if not group:
        summed = lax.all_gather(lax.psum(summed, ("row", "col")), "chan")
        summed = summed.reshape(chans, 2, local, 9 * channels)
    first, second = pl.pallas_call(
        write_kernel,
        out_shape=[shape((9, channels, channels), F32)] * 2,
        in_specs=[vmem()],
        out_specs=[vmem()] * 2,
        compiler_params=pltpu.CompilerParams(vmem_limit_bytes=16 * 1024 * 1024),
    )(summed)
    first = first.reshape(3, 3, channels, channels).transpose(2, 3, 0, 1)
    second = second.reshape(3, 3, channels, channels).transpose(2, 3, 0, 1)
    return grad_features, first, second


def solution(mesh):
    return jax.shard_map(
        functools.partial(body, dict(mesh.shape)),
        mesh=mesh,
        in_specs=(
            P(None, None, ("groups", "col"), "row"),
            P(None, "chan", ("groups", "col"), "row"),
            P("chan", None, ("groups", "col"), "row"),
            P("row", ("groups", "col")),
            P(),
            P(),
        ),
        out_specs=(
            P(None, "chan", ("groups", "col"), "row"),
            P("groups", None, None, None),
            P("groups", None, None, None),
        ),
        check_vma=False,
    )
```

```python
import functools
import math

import jax
import jax.numpy as jnp
from jax import lax
from jax.experimental import pallas as pl
from jax.experimental.pallas import tpu as pltpu
from jax.sharding import PartitionSpec as P

MAXOFF = 2
REACH = MAXOFF + 1
MESH = pl.DeviceIdType.MESH
SIDES = [(dr, dc) for dr in (-1, 1) for dc in (-1, 0, 1)]
F32 = jnp.float32
BF16 = jnp.bfloat16


def vmem():
    return pl.BlockSpec(memory_space=pltpu.VMEM)


def rolled(value, by):
    by = by % value.shape[-1]
    return value if by == 0 else pltpu.roll(value, by, value.ndim - 1)


def lane_index(shape):
    return lax.broadcasted_iota(jnp.int32, shape, len(shape) - 1)


def either(condition, value, lanes):
    start = jnp.where(condition, 0, lanes.shape[-1])
    return jnp.where(lanes >= start, value, 0.0)


class Links:
    def __init__(self, sizes, send_sem, recv_sem):
        self.sizes = sizes
        self.at = {axis: lax.axis_index(axis) for axis in sizes}
        self.send_sem, self.recv_sem = send_sem, recv_sem
        self.used = 0

    def exists(self, move):
        found = None
        for axis, by in move.items():
            if axis == "chan" or by == 0:
                continue
            there = self.at[axis] + by
            here = jnp.logical_and(there >= 0, there < self.sizes[axis])
            found = here if found is None else jnp.logical_and(found, here)
        return found

    def where(self, move):
        return {
            axis: lax.rem(self.at[axis] + (by + self.sizes[axis]), self.sizes[axis])
            for axis, by in move.items()
        }

    def when(self, move, action):
        found = self.exists(move)
        if found is None:
            action()
        else:
            pl.when(found)(action)

    def back(self, move):
        return {axis: -by for axis, by in move.items()}

    def greet(self, moves, group):
        barrier = pltpu.get_barrier_semaphore()
        count = 0
        for move in moves:
            origin = self.back(move)
            self.when(
                origin,
                lambda origin=origin: pl.semaphore_signal(
                    barrier, inc=1, device_id=self.where(origin), device_id_type=MESH
                ),
            )
            found = self.exists(move)
            count = count + (1 if found is None else found.astype(jnp.int32))
        for by in range(1, group):
            device = self.peer(-by, group)[1]
            pl.semaphore_signal(barrier, inc=1, device_id=device, device_id_type=MESH)
            count = count + 1
        pl.semaphore_wait(barrier, count)

    def peer(self, by, group):
        cols = self.sizes["col"]
        me = self.at["row"] * cols + self.at["col"]
        rank = lax.rem(me + by + group, group)
        return rank, {"row": lax.div(rank, cols), "col": lax.rem(rank, cols)}

    def copy(self, src, dst, device):
        at = self.used
        self.used += 1
        return pltpu.make_async_remote_copy(
            src_ref=src,
            dst_ref=dst,
            send_sem=self.send_sem.at[at],
            recv_sem=self.recv_sem.at[at],
            device_id=device,
            device_id_type=MESH,
        )

    def send(self, move, src, dst):
        copy = self.copy(src, dst, self.where(move))
        self.when(move, copy.start)
        return move, copy

    def received(self, sent):
        for move, copy in sent:
            self.when(self.back(move), copy.wait_recv)

    def left(self, sent):
        for move, copy in sent:
            self.when(move, copy.wait_send)


def packed_edges(tiles, per):
    count = len(tiles)
    rows = tiles[0].shape[0] // per
    lanes = lane_index((rows, tiles[0].shape[1]))
    packed = jnp.zeros(lanes.shape, F32)
    for q in range(per):
        first = q * 2 * count
        for k, tile in enumerate(tiles):
            piece = tile[q * rows : (q + 1) * rows]
            packed = jnp.where(lanes == first + k, rolled(piece, first + k + 1), packed)
            packed = jnp.where(
                lanes == first + count + k, rolled(piece, first + count + k), packed
            )
    return packed


def spread(blocks, by, per, count):
    return jnp.concatenate(
        [rolled(block, by - q * 2 * count) for block in blocks for q in range(per)], axis=0
    )


def fill_views(views, links, n, tile_of, side_of, edges_of, tile_w, lanes, per, count, first):
    width = lanes.shape[1]
    for dc in (-1, 0, 1):
        before = edges_of(SIDES.index((-1, dc)))
        after = edges_of(SIDES.index((1, dc)))
        slim = lane_index(before[0].shape)
        before = [either(links.exists({"row": -1, "col": dc}), b, slim) for b in before]
        after = [either(links.exists({"row": 1, "col": dc}), b, slim) for b in after]
        for xx in {-1: [0], 0: range(1, tile_w + 1), 1: [tile_w + 1]}[dc]:
            if dc == 0:
                tile, k = tile_of(xx - 1), first + xx - 1
            else:
                tile = either(links.exists({"col": dc}), side_of(0 if dc < 0 else 1), lanes)
                k = first + (tile_w - 1 if dc < 0 else 0)
            left = jnp.where(lanes == 0, spread(before, -k, per, count), rolled(tile, 1))
            right = jnp.where(
                lanes == width - 1,
                spread(after, width - 1 - count - k, per, count),
                rolled(tile, -1),
            )
            views[n, xx, 0] = left.astype(BF16)
            views[n, xx, 1] = tile.astype(BF16)
            views[n, xx, 2] = right.astype(BF16)


EDGE_MOVES = [{"row": -dr, "col": -dc} for dr, dc in SIDES]
SIDE_MOVES = [{"col": 1}, {"col": -1}]


def whole_kernel(
    sizes, group, offset_ref, features_hbm, target_hbm, image_hbm, w1_hbm, w2_hbm,
    grad_out, sum_out,
    grad_ref, sum_ref, features_ref, target_ref, image_ref, w1_ref, w2_ref, far_out, far_in, far_back, far_home,
    image, image_pack, image_edges, image_side, image_views, hidden_s, w1, w2, turned, turned_w,
    window, main_s, spill_s, outgoing, arrived, own, rounded, full, grad_pack, grad_edges,
    grad_side, grad_views, part, parts, send_sem, recv_sem, load_sem,
):
    links = Links(sizes, send_sem, recv_sem)
    images, channels, tile_w, width = image_ref.shape
    local = features_ref.shape[1]
    groups, disp = target_ref.shape[:2]
    size = local // groups
    inv = 1.0 / size
    chans = sizes["chan"]
    chan = links.at["chan"]
    row = links.at["row"]
    direct = group > 0
    forward = [{"row": k} for k in range(1, REACH + 1)]
    backward = [{"row": -k} for k in range(1, REACH + 1)]
    with_chan = [{**move, "chan": c} for move in EDGE_MOVES + SIDE_MOVES for c in range(chans)]
    partners = [{"chan": c} for c in range(1, chans)]
    loads = [
        pltpu.make_async_copy(src, dst, load_sem.at[i])
        for i, (src, dst) in enumerate([
            (features_hbm.at[1], features_ref.at[1]),
            (image_hbm, image_ref),
            (w1_hbm, w1_ref),
            (w2_hbm, w2_ref),
            (features_hbm.at[0], features_ref.at[0]),
            (target_hbm, target_ref),
        ])
    ]
    for load in loads:
        load.start()
    pending = []
    lanes = lane_index((channels, width))
    small = lane_index((tile_w, width))
    abreast = width // disp

    def packed_far(values, dst, first):
        for i in range(first, first + -(-size // abreast)):
            packed = None
            for r in range(abreast):
                c = (i - first) * abreast + r
                if c < size:
                    value = rolled(values[c], disp + r * disp)
                    packed = value if r == 0 else jnp.where(small >= r * disp, value, packed)
            dst[i] = packed.astype(BF16)

    def unpacked_far(src, first):
        return jnp.stack([
            rolled(src[first + c // abreast].astype(F32), width - disp - (c % abreast) * disp)
            for c in range(size)
        ])

    far = -(-size // abreast)

    def far_of(g):
        return pl.ds(g * far, far)

    loads[0].wait()
    for g in range(groups):
        packed_far(features_ref[1, g * size : (g + 1) * size].astype(F32), far_out, g * far)
    links.greet(forward + backward + with_chan + partners, group)

    def parts_of(g):
        return pl.ds(g * size, size)

    fetched = []
    for g in range(groups):
        fetched.append([
            links.send(
                forward[k], features_ref.at[1, parts_of(g)], window.at[k, parts_of(g)]
            )
            for k in range(MAXOFF)
        ])
        fetched[-1].append(
            links.send(forward[MAXOFF], far_out.at[far_of(g)], far_in.at[far_of(g)])
        )
        pending += fetched[-1]

    loads[1].wait()
    for n in range(images):
        turned[...] = image_ref[n].astype(F32)
        for x in range(tile_w):
            image[n, x] = turned[:, x, :].astype(BF16)
    border = [
        links.send(move, image.at[:, x], image_side.at[side])
        for side, (x, move) in enumerate(zip((tile_w - 1, 0), SIDE_MOVES))
    ]
    count = images * tile_w
    image_per = channels // image_pack.shape[0]
    image_pack[...] = packed_edges(
        [image[n, x].astype(F32) for n in range(images) for x in range(tile_w)], image_per
    ).astype(BF16)
    border += [
        links.send(move, image_pack, image_edges.at[j]) for j, move in enumerate(EDGE_MOVES)
    ]
    pending += border

    loads[2].wait()
    loads[3].wait()
    first_ch = pl.multiple_of(chan * local, local)
    mine = pl.ds(first_ch, local)
    taps = [(a, b) for a in range(3) for b in range(3)]
    w1[...] = jnp.concatenate([w1_ref[a, b, mine].astype(F32) for a, b in taps], axis=1).astype(BF16)
    flipped = jnp.concatenate([w2_ref[2 - a, 2 - b].astype(F32) for a, b in taps], axis=0)
    turned_w[...] = flipped.T
    w2[...] = turned_w[mine].astype(BF16)

    links.received(border)
    for n in range(images):
        fill_views(
            image_views, links, n,
            lambda x, n=n: image[n, x].astype(F32),
            lambda side, n=n: image_side[side, n].astype(F32),
            lambda j: [image_edges[j].astype(F32)],
            tile_w, lanes, image_per, count, n * tile_w,
        )
    for n in range(images):
        for x in range(tile_w):
            view = image_views[n, x : x + 3].reshape(9 * channels, width)
            total = jnp.dot(w1[...], view, preferred_element_type=F32)
            hidden_s[n, x] = jnp.maximum(total, 0.0).astype(BF16)

    loads[4].wait()
    loads[5].wait()
    offset = jnp.broadcast_to(offset_ref[...], (tile_w, width))
    inside = small * 0 + row
    main_in = [offset == k for k in range(REACH)]
    spill_in = [
        jnp.logical_and(offset + 1 == k, inside >= k) for k in range(1, REACH + 1)
    ]
    returned = []
    for g in range(groups):
        links.received(fetched[g])
        chosen = parts_of(g)
        main = jnp.where(main_in[0], features_ref[1, chosen].astype(F32), 0.0)
        spill = jnp.zeros_like(main)
        for k in range(REACH):
            got = window[k, chosen].astype(F32) if k < MAXOFF else unpacked_far(far_in, g * far)
            spill = jnp.where(spill_in[k], got, spill)
            if k + 1 < REACH:
                main = jnp.where(main_in[k + 1], got, main)
        main_s[...] = main
        spill_s[...] = spill

        def step(t, state, g=g, chosen=chosen):
            left_grad, main_grad, spill_grad = state
            left = features_ref[0, chosen].astype(F32)
            for j in range(8):
                d = t * 8 + j
                keep = small < width - d
                shifted = pltpu.roll(jnp.where(keep, main_s[...], spill_s[...]), d, 2)
                volume = jnp.sum(left * shifted, axis=0) * inv
                weighted = (volume - target_ref[g, d].astype(F32)) * inv
                left_grad = left_grad + weighted * shifted
                back = pltpu.roll(weighted * left, lax.rem(width - d, width), 2)
                main_grad = main_grad + jnp.where(keep, back, 0.0)
                spill_grad = spill_grad + jnp.where(keep, 0.0, back)
            return left_grad, main_grad, spill_grad

        zero = jnp.zeros((size, tile_w, width), F32)
        left_grad, main_grad, spill_grad = lax.fori_loop(0, disp // 8, step, (zero, zero, zero))
        for k in range(1, REACH + 1):
            piece = jnp.where(spill_in[k - 1], spill_grad, 0.0)
            if k < REACH:
                piece = jnp.where(main_in[k], main_grad, piece)
                outgoing[k - 1, chosen] = piece.astype(BF16)
            else:
                packed_far(piece, far_back, g * far)
        returned.append([
            links.send(backward[k], outgoing.at[k, chosen], arrived.at[k, chosen])
            for k in range(MAXOFF)
        ])
        returned[-1].append(
            links.send(backward[MAXOFF], far_back.at[far_of(g)], far_home.at[far_of(g)])
        )
        pending += returned[-1]
        own[chosen] = jnp.where(main_in[0], main_grad, 0.0)
        left_grad = left_grad.astype(BF16)
        grad_ref[0, chosen] = left_grad
        rounded[0, chosen] = left_grad.astype(F32)

    grad_per = local // grad_pack.shape[1]

    def share(n):
        for x in range(tile_w):
            full[n, chan, x] = rounded[n, :, x, :].astype(BF16)
        sent = [links.send(move, full.at[n, chan], full.at[n, chan]) for move in partners]
        for c in range(chans):
            for side, (x, move) in enumerate(zip((tile_w - 1, 0), SIDE_MOVES)):
                sent.append(links.send(
                    {**move, "chan": c}, full.at[n, chan, x], grad_side.at[n, side, chan]
                ))
        grad_pack[n] = packed_edges(
            [rounded[n, :, x, :] for x in range(tile_w)], grad_per
        ).astype(BF16)
        for c in range(chans):
            for j, move in enumerate(EDGE_MOVES):
                sent.append(links.send(
                    {**move, "chan": c}, grad_pack.at[n], grad_edges.at[n, j, chan]
                ))
        return sent

    def joined(pieces):
        return jnp.concatenate([p.astype(F32) for p in pieces], axis=0)

    contract = (((1,), (1,)), ((), ()))

    def gradients(n, first, second):
        fill_views(
            grad_views, links, n,
            lambda x: joined([full[n, c, x] for c in range(chans)]),
            lambda side: joined([grad_side[n, side, c] for c in range(chans)]),
            lambda j: [grad_edges[n, j, c].astype(F32) for c in range(chans)],
            tile_w, lanes, grad_per, tile_w, 0,
        )
        for x in range(tile_w):
            view = grad_views[n, x : x + 3].reshape(9 * channels, width)
            hidden = hidden_s[n, x]
            total = jnp.dot(w2[...], view, preferred_element_type=F32)
            hidden_grad = jnp.where(hidden.astype(F32) > 0, total, 0.0).astype(BF16)
            second += lax.dot_general(hidden, view, contract, preferred_element_type=F32)
            seen = image_views[n, x : x + 3].reshape(9 * channels, width)
            first += lax.dot_general(hidden_grad, seen, contract, preferred_element_type=F32)
        return first, second

    def save(src, dst, at):
        copy = pltpu.make_async_copy(src, dst, load_sem.at[at])
        copy.start()
        return copy

    saves = [save(grad_ref.at[0], grad_out.at[0], 6)]
    left_sent = share(0)
    for g in range(groups):
        links.received(returned[g])
        chosen = parts_of(g)
        right_grad = own[chosen]
        for k in range(REACH):
            there = inside + (k + 1) < sizes["row"]
            if k < MAXOFF:
                got = arrived[k, chosen].astype(F32)
            else:
                got = unpacked_far(far_home, g * far)
                there = jnp.logical_and(there, small >= width - disp)
            right_grad = right_grad + jnp.where(there, got, 0.0)
        right_grad = right_grad.astype(BF16)
        grad_ref[1, chosen] = right_grad
        rounded[1, chosen] = right_grad.astype(F32)
    saves.append(save(grad_ref.at[1], grad_out.at[1], 7))
    right_sent = share(1)
    pending += left_sent + right_sent
    empty = jnp.zeros((local, 9 * channels), F32)
    links.received(left_sent)
    first, second = gradients(0, empty, empty)
    links.received(right_sent)
    first, second = gradients(1, first, second)
    pixels = images * tile_w * sizes["col"] * width * sizes["row"]
    factor = 1.0 / math.sqrt(pixels)
    first, second = first * factor, second * factor

    if direct:
        rows = 2 * local // group
        half = group // 2
        for j in range(half):
            part[j] = first[j * rows : (j + 1) * rows].astype(BF16)
            part[half + j] = second[j * rows : (j + 1) * rows].astype(BF16)
        scattered, gathered, relayed = [], [], []
        for by in range(1, group):
            rank, device = links.peer(by, group)
            scattered.append(links.copy(part.at[rank], parts.at[by - 1], device))
            scattered[-1].start()
        me = links.peer(0, group)[0]
        total = part[me].astype(F32)
        for by in range(1, group):
            scattered[by - 1].wait_recv()
            total = total + parts[by - 1].astype(F32)
        sum_ref[chan, me] = total.astype(BF16)
        partner = links.where(partners[0])
        held = sum_ref.at[chan, me]
        for by in range(1, group):
            gathered.append(links.copy(held, held, links.peer(by, group)[1]))
            gathered[-1].start()
        relayed.append(links.copy(held, held, partner))
        relayed[-1].start()
        for by in range(1, group):
            gathered[by - 1].wait_recv()
            held = sum_ref.at[chan, links.peer(-by, group)[0]]
            relayed.append(links.copy(held, held, partner))
            relayed[-1].start()
        for copy in relayed:
            copy.wait_recv()
        saves.append(save(sum_ref, sum_out, 8))
        for copy in scattered + gathered + relayed:
            copy.wait_send()
    else:
        sum_ref[:local] = first
        sum_ref[local:] = second
        saves.append(save(sum_ref, sum_out, 8))
    links.left(pending)
    for copy in saves:
        copy.wait()


def write_kernel(grad_ref, sum_ref, out_ref, first_ref, second_ref, sem):
    copy = pltpu.make_async_copy(grad_ref, out_ref, sem)
    copy.start()
    chans, pieces = sum_ref.shape[:2]
    channels = first_ref.shape[1]
    half = pieces // 2

    def rows(pick):
        return jnp.concatenate(
            [sum_ref[c, j].astype(F32) for c in range(chans) for j in pick], axis=0
        )

    first = rows(range(half))
    second = rows(range(half, pieces)).T
    for t in range(9):
        chosen = slice(t * channels, (t + 1) * channels)
        first_ref[t] = first[:, chosen]
        second_ref[8 - t] = second[chosen]
    copy.wait()


def body(sizes, layer_input, features, vol_target, offsets, w_first, w_second):
    images, channels, tile_w, width = layer_input.shape
    local = features.shape[1]
    chans = sizes["chan"]
    shape = jax.ShapeDtypeStruct
    dma = pltpu.SemaphoreType.DMA
    scratch = pltpu.VMEM
    size = local // vol_target.shape[0]
    group = sizes["row"] * sizes["col"]
    if chans != 2 or group % 2 or (2 * local) % (8 * group):
        group = 0
    rows = 2 * local // max(group, 2)
    views = (images, tile_w + 2, 3, channels, width)
    tile = (local, tile_w, width)
    image_per = min(width // (2 * images * tile_w), channels // 16)
    grad_per = min(width // (2 * tile_w), local // 8)
    far = vol_target.shape[0] * -(-size // (width // vol_target.shape[1]))
    count = 2 * REACH * vol_target.shape[0] + 2 + len(SIDES)
    count += images * ((chans - 1) + chans * (2 + len(SIDES))) + 3 * group
    if group:
        summed_shape = shape((chans, group, rows, 9 * channels), BF16)
    else:
        summed_shape = shape((2 * local, 9 * channels), F32)
    grad_features, summed = pl.pallas_call(
        functools.partial(whole_kernel, sizes, group),
        out_shape=[shape((2,) + tile, BF16), summed_shape],
        in_specs=[vmem()] + [pl.BlockSpec(memory_space=pl.ANY)] * 5,
        out_specs=[pl.BlockSpec(memory_space=pl.ANY)] * 2,
        scratch_shapes=[
            scratch((2,) + tile, BF16),
            scratch(summed_shape.shape, summed_shape.dtype),
            scratch(features.shape, BF16),
            scratch(vol_target.shape, BF16),
            scratch(layer_input.shape, BF16),
            scratch((3, 3, channels, channels), BF16),
            scratch((3, 3, channels, channels), BF16),
            scratch((far, tile_w, width), BF16),
            scratch((far, tile_w, width), BF16),
            scratch((far, tile_w, width), BF16),
            scratch((far, tile_w, width), BF16),
            scratch((images, tile_w, channels, width), BF16),
            scratch((channels // image_per, width), BF16),
            scratch((len(SIDES), channels // image_per, width), BF16),
            scratch((2, images, channels, width), BF16),
            scratch(views, BF16),
            scratch((images, tile_w, local, width), BF16),
            scratch((local, 9 * channels), BF16),
            scratch((local, 9 * channels), BF16),
            scratch((channels, tile_w, width), F32),
            scratch((channels, 9 * channels), F32),
            scratch((MAXOFF,) + tile, BF16),
            scratch((size, tile_w, width), F32),
            scratch((size, tile_w, width), F32),
            scratch((MAXOFF,) + tile, BF16),
            scratch((MAXOFF,) + tile, BF16),
            scratch(tile, F32),
            scratch((2,) + tile, F32),
            scratch((2, chans, tile_w, local, width), BF16),
            scratch((2, local // grad_per, width), BF16),
            scratch((2, len(SIDES), chans, local // grad_per, width), BF16),
            scratch((2, 2, chans, local, width), BF16),
            scratch(views, BF16),
            scratch((max(group, 2), rows, 9 * channels), BF16),
            scratch((max(group, 2), rows, 9 * channels), BF16),
            dma((count,)),
            dma((count,)),
            dma((9,)),
        ],
        compiler_params=pltpu.CompilerParams(
            collective_id=0, has_side_effects=True, vmem_limit_bytes=60 * 1024 * 1024
        ),
    )(
        offsets,
        features,
        vol_target,
        layer_input,
        w_first.transpose(2, 3, 0, 1),
        w_second.transpose(2, 3, 0, 1),
    )
    if not group:
        summed = lax.all_gather(lax.psum(summed, ("row", "col")), "chan")
        summed = summed.reshape(chans, 2, local, 9 * channels)
    grad_features, first, second = pl.pallas_call(
        write_kernel,
        out_shape=[shape((2,) + tile, BF16)] + [shape((9, channels, channels), F32)] * 2,
        in_specs=[pl.BlockSpec(memory_space=pl.ANY), vmem()],
        out_specs=[pl.BlockSpec(memory_space=pl.ANY)] + [vmem()] * 2,
        scratch_shapes=[dma],
        compiler_params=pltpu.CompilerParams(vmem_limit_bytes=60 * 1024 * 1024),
    )(grad_features, summed)
    first = first.reshape(3, 3, channels, channels).transpose(2, 3, 0, 1)
    second = second.reshape(3, 3, channels, channels).transpose(2, 3, 0, 1)
    return grad_features, first, second


def solution(mesh):
    return jax.shard_map(
        functools.partial(body, dict(mesh.shape)),
        mesh=mesh,
        in_specs=(
            P(None, None, ("groups", "col"), "row"),
            P(None, "chan", ("groups", "col"), "row"),
            P("chan", None, ("groups", "col"), "row"),
            P("row", ("groups", "col")),
            P(),
            P(),
        ),
        out_specs=(
            P(None, "chan", ("groups", "col"), "row"),
            P("groups", None, None, None),
            P("groups", None, None, None),
        ),
        check_vma=False,
    )
```

```python
import functools
import math

import jax
import jax.numpy as jnp
from jax import lax
from jax.experimental import pallas as pl
from jax.experimental.pallas import tpu as pltpu
from jax.sharding import PartitionSpec as P

MAXOFF = 2
REACH = MAXOFF + 1
MESH = pl.DeviceIdType.MESH
SIDES = [(dr, dc) for dr in (-1, 1) for dc in (-1, 0, 1)]
F32 = jnp.float32
BF16 = jnp.bfloat16


def vmem():
    return pl.BlockSpec(memory_space=pltpu.VMEM)


def rolled(value, by):
    by = by % value.shape[-1]
    return value if by == 0 else pltpu.roll(value, by, value.ndim - 1)


def lane_index(shape):
    return lax.broadcasted_iota(jnp.int32, shape, len(shape) - 1)


def either(condition, value, lanes):
    start = jnp.where(condition, 0, lanes.shape[-1])
    return jnp.where(lanes >= start, value, 0.0)


class Links:
    def __init__(self, sizes, send_sem, recv_sem):
        self.sizes = sizes
        self.at = {axis: lax.axis_index(axis) for axis in sizes}
        self.send_sem, self.recv_sem = send_sem, recv_sem
        self.used = 0

    def exists(self, move):
        found = None
        for axis, by in move.items():
            if axis == "chan" or by == 0:
                continue
            there = self.at[axis] + by
            here = jnp.logical_and(there >= 0, there < self.sizes[axis])
            found = here if found is None else jnp.logical_and(found, here)
        return found

    def where(self, move):
        return {
            axis: lax.rem(self.at[axis] + (by + self.sizes[axis]), self.sizes[axis])
            for axis, by in move.items()
        }

    def when(self, move, action):
        found = self.exists(move)
        if found is None:
            action()
        else:
            pl.when(found)(action)

    def back(self, move):
        return {axis: -by for axis, by in move.items()}

    def greet(self, moves, group):
        barrier = pltpu.get_barrier_semaphore()
        count = 0
        for move in moves:
            origin = self.back(move)
            self.when(
                origin,
                lambda origin=origin: pl.semaphore_signal(
                    barrier, inc=1, device_id=self.where(origin), device_id_type=MESH
                ),
            )
            found = self.exists(move)
            count = count + (1 if found is None else found.astype(jnp.int32))
        for by in range(1, group):
            device = self.peer(-by, group)[1]
            pl.semaphore_signal(barrier, inc=1, device_id=device, device_id_type=MESH)
            count = count + 1
        return count

    def greeted(self, count):
        pl.semaphore_wait(pltpu.get_barrier_semaphore(), count)

    def peer(self, by, group):
        cols = self.sizes["col"]
        me = self.at["row"] * cols + self.at["col"]
        rank = lax.rem(me + by + group, group)
        return rank, {"row": lax.div(rank, cols), "col": lax.rem(rank, cols)}

    def copy(self, src, dst, device):
        at = self.used
        self.used += 1
        return pltpu.make_async_remote_copy(
            src_ref=src,
            dst_ref=dst,
            send_sem=self.send_sem.at[at],
            recv_sem=self.recv_sem.at[at],
            device_id=device,
            device_id_type=MESH,
        )

    def send(self, move, src, dst):
        copy = self.copy(src, dst, self.where(move))
        self.when(move, copy.start)
        return move, copy

    def received(self, sent):
        for move, copy in sent:
            self.when(self.back(move), copy.wait_recv)

    def left(self, sent):
        for move, copy in sent:
            self.when(move, copy.wait_send)


def packed_edges(tiles, per):
    count = len(tiles)
    rows = tiles[0].shape[0] // per
    lanes = lane_index((rows, tiles[0].shape[1]))
    packed = jnp.zeros(lanes.shape, F32)
    for q in range(per):
        first = q * 2 * count
        for k, tile in enumerate(tiles):
            piece = tile[q * rows : (q + 1) * rows]
            packed = jnp.where(lanes == first + k, rolled(piece, first + k + 1), packed)
            packed = jnp.where(
                lanes == first + count + k, rolled(piece, first + count + k), packed
            )
    return packed


def spread(blocks, by, per, count):
    return jnp.concatenate(
        [rolled(block, by - q * 2 * count) for block in blocks for q in range(per)], axis=0
    )


def fill_views(views, links, n, tile_of, side_of, edges_of, tile_w, lanes, per, count, first):
    width = lanes.shape[1]
    for dc in (-1, 0, 1):
        before = edges_of(SIDES.index((-1, dc)))
        after = edges_of(SIDES.index((1, dc)))
        slim = lane_index(before[0].shape)
        before = [either(links.exists({"row": -1, "col": dc}), b, slim) for b in before]
        after = [either(links.exists({"row": 1, "col": dc}), b, slim) for b in after]
        for xx in {-1: [0], 0: range(1, tile_w + 1), 1: [tile_w + 1]}[dc]:
            if dc == 0:
                tile, k = tile_of(xx - 1), first + xx - 1
            else:
                tile = either(links.exists({"col": dc}), side_of(0 if dc < 0 else 1), lanes)
                k = first + (tile_w - 1 if dc < 0 else 0)
            left = jnp.where(lanes == 0, spread(before, -k, per, count), rolled(tile, 1))
            right = jnp.where(
                lanes == width - 1,
                spread(after, width - 1 - count - k, per, count),
                rolled(tile, -1),
            )
            views[n, xx, 0] = left.astype(BF16)
            views[n, xx, 1] = tile.astype(BF16)
            views[n, xx, 2] = right.astype(BF16)


EDGE_MOVES = [{"row": -dr, "col": -dc} for dr, dc in SIDES]
SIDE_MOVES = [{"col": 1}, {"col": -1}]


def whole_kernel(
    sizes, group, offset_ref, features_hbm, target_hbm, image_hbm, w1_hbm, w2_hbm,
    grad_out, sum_out,
    grad_ref, sum_ref, features_ref, target_ref, image_ref, w1_ref, w2_ref, far_out, far_in, far_back, far_home,
    image, image_pack, image_edges, image_side, image_views, hidden_s, w1, w2, turned, turned_w,
    window, main_s, spill_s, outgoing, arrived, own, rounded, full, grad_pack, grad_edges,
    grad_side, grad_views, part, parts, send_sem, recv_sem, load_sem,
):
    links = Links(sizes, send_sem, recv_sem)
    images, channels, tile_w, width = image_ref.shape
    local = features_ref.shape[1]
    groups, disp = target_ref.shape[:2]
    size = local // groups
    inv = 1.0 / size
    chans = sizes["chan"]
    chan = links.at["chan"]
    row = links.at["row"]
    direct = group > 0
    forward = [{"row": k} for k in range(1, REACH + 1)]
    backward = [{"row": -k} for k in range(1, REACH + 1)]
    with_chan = [{**move, "chan": c} for move in EDGE_MOVES + SIDE_MOVES for c in range(chans)]
    partners = [{"chan": c} for c in range(1, chans)]
    met = with_chan + partners
    if direct:
        met = [move for move in met if move["chan"]]
    else:
        met = met + forward + backward
    loads = [
        pltpu.make_async_copy(src, dst, load_sem.at[i])
        for i, (src, dst) in enumerate([
            (features_hbm.at[1], features_ref.at[1]),
            (image_hbm, image_ref),
            (w1_hbm, w1_ref),
            (w2_hbm, w2_ref),
            (features_hbm.at[0], features_ref.at[0]),
            (target_hbm, target_ref),
        ])
    ]
    for load in loads:
        load.start()
    expected = links.greet(met, group)
    pending = []
    lanes = lane_index((channels, width))
    small = lane_index((tile_w, width))
    abreast = width // disp

    def packed_far(values, dst, first):
        for i in range(first, first + -(-size // abreast)):
            packed = None
            for r in range(abreast):
                c = (i - first) * abreast + r
                if c < size:
                    value = rolled(values[c], disp + r * disp)
                    packed = value if r == 0 else jnp.where(small >= r * disp, value, packed)
            dst[i] = packed.astype(BF16)

    def unpacked_far(src, first):
        return jnp.stack([
            rolled(src[first + c // abreast].astype(F32), width - disp - (c % abreast) * disp)
            for c in range(size)
        ])

    far = -(-size // abreast)

    def far_of(g):
        return pl.ds(g * far, far)

    loads[0].wait()
    for g in range(groups):
        packed_far(features_ref[1, g * size : (g + 1) * size].astype(F32), far_out, g * far)

    loads[1].wait()
    for n in range(images):
        turned[...] = image_ref[n].astype(F32)
        for x in range(tile_w):
            image[n, x] = turned[:, x, :].astype(BF16)
    count = images * tile_w
    image_per = channels // image_pack.shape[0]
    image_pack[...] = packed_edges(
        [image[n, x].astype(F32) for n in range(images) for x in range(tile_w)], image_per
    ).astype(BF16)
    links.greeted(expected)

    def parts_of(g):
        return pl.ds(g * size, size)

    fetched = {}
    chunk = groups // 2 if groups % 2 == 0 else groups

    def fetch(g):
        chosen = pl.ds(g * size, chunk * size)
        far_chosen = pl.ds(g * far, chunk * far)
        fetched[g] = [
            links.send(move, features_ref.at[1, chosen], window.at[k, chosen])
            for k, move in enumerate(forward[:MAXOFF])
        ]
        fetched[g].append(
            links.send(forward[MAXOFF], far_out.at[far_chosen], far_in.at[far_chosen])
        )
        pending.extend(fetched[g])

    fetch(0)
    border = [
        links.send(move, image.at[:, x], image_side.at[side])
        for side, (x, move) in enumerate(zip((tile_w - 1, 0), SIDE_MOVES))
    ]
    border += [
        links.send(move, image_pack, image_edges.at[j]) for j, move in enumerate(EDGE_MOVES)
    ]
    pending += border
    for g in range(chunk, groups, chunk):
        fetch(g)

    loads[2].wait()
    loads[3].wait()
    first_ch = pl.multiple_of(chan * local, local)
    mine = pl.ds(first_ch, local)
    taps = [(a, b) for a in range(3) for b in range(3)]
    w1[...] = jnp.concatenate([w1_ref[a, b, mine].astype(F32) for a, b in taps], axis=1).astype(BF16)
    flipped = jnp.concatenate([w2_ref[2 - a, 2 - b].astype(F32) for a, b in taps], axis=0)
    turned_w[...] = flipped.T
    w2[...] = turned_w[mine].astype(BF16)

    links.received(border)
    for n in range(images):
        fill_views(
            image_views, links, n,
            lambda x, n=n: image[n, x].astype(F32),
            lambda side, n=n: image_side[side, n].astype(F32),
            lambda j: [image_edges[j].astype(F32)],
            tile_w, lanes, image_per, count, n * tile_w,
        )

    loads[4].wait()
    loads[5].wait()
    offset = jnp.broadcast_to(offset_ref[...], (tile_w, width))
    inside = small * 0 + row
    main_in = [offset == k for k in range(REACH)]
    spill_in = [
        jnp.logical_and(offset + 1 == k, inside >= k) for k in range(1, REACH + 1)
    ]
    returned = []
    for g in range(groups):
        links.received(fetched.get(g, []))
        chosen = parts_of(g)
        main = jnp.where(main_in[0], features_ref[1, chosen].astype(F32), 0.0)
        spill = jnp.zeros_like(main)
        for k in range(REACH):
            got = window[k, chosen].astype(F32) if k < MAXOFF else unpacked_far(far_in, g * far)
            spill = jnp.where(spill_in[k], got, spill)
            if k + 1 < REACH:
                main = jnp.where(main_in[k + 1], got, main)
        main_s[...] = main
        spill_s[...] = spill

        def step(t, state, g=g, chosen=chosen):
            left_grad, main_grad, spill_grad = state
            left = features_ref[0, chosen].astype(F32)
            for j in range(8):
                d = t * 8 + j
                keep = small < width - d
                shifted = pltpu.roll(jnp.where(keep, main_s[...], spill_s[...]), d, 2)
                volume = jnp.sum(left * shifted, axis=0) * inv
                weighted = (volume - target_ref[g, d].astype(F32)) * inv
                left_grad = left_grad + weighted * shifted
                back = pltpu.roll(weighted * left, lax.rem(width - d, width), 2)
                main_grad = main_grad + jnp.where(keep, back, 0.0)
                spill_grad = spill_grad + jnp.where(keep, 0.0, back)
            return left_grad, main_grad, spill_grad

        zero = jnp.zeros((size, tile_w, width), F32)
        left_grad, main_grad, spill_grad = lax.fori_loop(0, disp // 8, step, (zero, zero, zero))
        for k in range(1, REACH + 1):
            piece = jnp.where(spill_in[k - 1], spill_grad, 0.0)
            if k < REACH:
                piece = jnp.where(main_in[k], main_grad, piece)
                outgoing[k - 1, chosen] = piece.astype(BF16)
            else:
                packed_far(piece, far_back, g * far)
        returned.append([
            links.send(backward[k], outgoing.at[k, chosen], arrived.at[k, chosen])
            for k in range(MAXOFF)
        ])
        returned[-1].append(
            links.send(backward[MAXOFF], far_back.at[far_of(g)], far_home.at[far_of(g)])
        )
        pending += returned[-1]
        own[chosen] = jnp.where(main_in[0], main_grad, 0.0)
        left_grad = left_grad.astype(BF16)
        grad_ref[0, chosen] = left_grad
        rounded[0, chosen] = left_grad.astype(F32)

    grad_per = local // grad_pack.shape[1]

    def share(n):
        for x in range(tile_w):
            full[n, chan, x] = rounded[n, :, x, :].astype(BF16)
        sent = [links.send(move, full.at[n, chan], full.at[n, chan]) for move in partners]
        for c in range(chans):
            for side, (x, move) in enumerate(zip((tile_w - 1, 0), SIDE_MOVES)):
                sent.append(links.send(
                    {**move, "chan": c}, full.at[n, chan, x], grad_side.at[n, side, chan]
                ))
        grad_pack[n] = packed_edges(
            [rounded[n, :, x, :] for x in range(tile_w)], grad_per
        ).astype(BF16)
        for c in range(chans):
            for j, move in enumerate(EDGE_MOVES):
                sent.append(links.send(
                    {**move, "chan": c}, grad_pack.at[n], grad_edges.at[n, j, chan]
                ))
        return sent

    def joined(pieces):
        return jnp.concatenate([p.astype(F32) for p in pieces], axis=0)

    contract = (((1,), (1,)), ((), ()))

    def gradients(n, first, second):
        fill_views(
            grad_views, links, n,
            lambda x: joined([full[n, c, x] for c in range(chans)]),
            lambda side: joined([grad_side[n, side, c] for c in range(chans)]),
            lambda j: [grad_edges[n, j, c].astype(F32) for c in range(chans)],
            tile_w, lanes, grad_per, tile_w, 0,
        )
        for x in range(tile_w):
            view = grad_views[n, x : x + 3].reshape(9 * channels, width)
            hidden = hidden_s[n, x]
            total = jnp.dot(w2[...], view, preferred_element_type=F32)
            hidden_grad = jnp.where(hidden.astype(F32) > 0, total, 0.0).astype(BF16)
            second += lax.dot_general(hidden, view, contract, preferred_element_type=F32)
            seen = image_views[n, x : x + 3].reshape(9 * channels, width)
            first += lax.dot_general(hidden_grad, seen, contract, preferred_element_type=F32)
        return first, second

    def save(src, dst, at):
        copy = pltpu.make_async_copy(src, dst, load_sem.at[at])
        copy.start()
        return copy

    saves = [save(grad_ref.at[0], grad_out.at[0], 6)]
    left_sent = share(0)
    for n in range(images):
        for x in range(tile_w):
            view = image_views[n, x : x + 3].reshape(9 * channels, width)
            total = jnp.dot(w1[...], view, preferred_element_type=F32)
            hidden_s[n, x] = jnp.maximum(total, 0.0).astype(BF16)
    for g in range(groups):
        links.received(returned[g])
        chosen = parts_of(g)
        right_grad = own[chosen]
        for k in range(REACH):
            there = inside + (k + 1) < sizes["row"]
            if k < MAXOFF:
                got = arrived[k, chosen].astype(F32)
            else:
                got = unpacked_far(far_home, g * far)
                there = jnp.logical_and(there, small >= width - disp)
            right_grad = right_grad + jnp.where(there, got, 0.0)
        right_grad = right_grad.astype(BF16)
        grad_ref[1, chosen] = right_grad
        rounded[1, chosen] = right_grad.astype(F32)
    saves.append(save(grad_ref.at[1], grad_out.at[1], 7))
    right_sent = share(1)
    pending += left_sent + right_sent
    empty = jnp.zeros((local, 9 * channels), F32)
    links.received(left_sent)
    first, second = gradients(0, empty, empty)
    links.received(right_sent)
    first, second = gradients(1, first, second)
    pixels = images * tile_w * sizes["col"] * width * sizes["row"]
    factor = 1.0 / math.sqrt(pixels)
    first, second = first * factor, second * factor

    if direct:
        rows = 2 * local // group
        half = group // 2
        for j in range(half):
            part[j] = first[j * rows : (j + 1) * rows].astype(BF16)
            part[half + j] = second[j * rows : (j + 1) * rows].astype(BF16)
        scattered, gathered, relayed = [], [], []
        for by in range(1, group):
            rank, device = links.peer(by, group)
            scattered.append(links.copy(part.at[rank], parts.at[by - 1], device))
            scattered[-1].start()
        links.left(pending)
        me = links.peer(0, group)[0]
        total = part[me].astype(F32)
        for by in range(1, group):
            scattered[by - 1].wait_recv()
            total = total + parts[by - 1].astype(F32)
        sum_ref[chan, me] = total.astype(BF16)
        partner = links.where(partners[0])
        held = sum_ref.at[chan, me]
        for by in range(1, group):
            gathered.append(links.copy(held, held, links.peer(by, group)[1]))
            gathered[-1].start()
        relayed.append(links.copy(held, held, partner))
        relayed[-1].start()
        for by in range(1, group):
            gathered[by - 1].wait_recv()
            held = sum_ref.at[chan, links.peer(-by, group)[0]]
            relayed.append(links.copy(held, held, partner))
            relayed[-1].start()
        for copy in relayed:
            copy.wait_recv()
        saves.append(save(sum_ref, sum_out, 8))
        for copy in scattered + gathered + relayed:
            copy.wait_send()
    else:
        sum_ref[:local] = first
        sum_ref[local:] = second
        saves.append(save(sum_ref, sum_out, 8))
        links.left(pending)
    for copy in saves:
        copy.wait()


def write_kernel(grad_ref, sum_ref, out_ref, first_ref, second_ref):
    out_ref[...] = grad_ref[...]
    chans, pieces = sum_ref.shape[:2]
    channels = first_ref.shape[1]
    half = pieces // 2

    def rows(pick):
        return jnp.concatenate(
            [sum_ref[c, j].astype(F32) for c in range(chans) for j in pick], axis=0
        )

    first = rows(range(half))
    second = rows(range(half, pieces)).T
    for t in range(9):
        chosen = slice(t * channels, (t + 1) * channels)
        first_ref[t] = first[:, chosen]
        second_ref[8 - t] = second[chosen]


def body(sizes, layer_input, features, vol_target, offsets, w_first, w_second):
    images, channels, tile_w, width = layer_input.shape
    local = features.shape[1]
    chans = sizes["chan"]
    shape = jax.ShapeDtypeStruct
    dma = pltpu.SemaphoreType.DMA
    scratch = pltpu.VMEM
    size = local // vol_target.shape[0]
    group = sizes["row"] * sizes["col"]
    if chans != 2 or group % 2 or (2 * local) % (8 * group):
        group = 0
    rows = 2 * local // max(group, 2)
    views = (images, tile_w + 2, 3, channels, width)
    tile = (local, tile_w, width)
    image_per = min(width // (2 * images * tile_w), channels // 16)
    grad_per = min(width // (2 * tile_w), local // 8)
    far = vol_target.shape[0] * -(-size // (width // vol_target.shape[1]))
    count = 2 * REACH * vol_target.shape[0] + 2 + len(SIDES)
    count += images * ((chans - 1) + chans * (2 + len(SIDES))) + 3 * group
    if group:
        summed_shape = shape((chans, group, rows, 9 * channels), BF16)
    else:
        summed_shape = shape((2 * local, 9 * channels), F32)
    grad_features, summed = pl.pallas_call(
        functools.partial(whole_kernel, sizes, group),
        out_shape=[shape((2,) + tile, BF16), summed_shape],
        in_specs=[vmem()] + [pl.BlockSpec(memory_space=pl.ANY)] * 5,
        out_specs=[pl.BlockSpec(memory_space=pl.ANY)] * 2,
        scratch_shapes=[
            scratch((2,) + tile, BF16),
            scratch(summed_shape.shape, summed_shape.dtype),
            scratch(features.shape, BF16),
            scratch(vol_target.shape, BF16),
            scratch(layer_input.shape, BF16),
            scratch((3, 3, channels, channels), BF16),
            scratch((3, 3, channels, channels), BF16),
            scratch((far, tile_w, width), BF16),
            scratch((far, tile_w, width), BF16),
            scratch((far, tile_w, width), BF16),
            scratch((far, tile_w, width), BF16),
            scratch((images, tile_w, channels, width), BF16),
            scratch((channels // image_per, width), BF16),
            scratch((len(SIDES), channels // image_per, width), BF16),
            scratch((2, images, channels, width), BF16),
            scratch(views, BF16),
            scratch((images, tile_w, local, width), BF16),
            scratch((local, 9 * channels), BF16),
            scratch((local, 9 * channels), BF16),
            scratch((channels, tile_w, width), F32),
            scratch((channels, 9 * channels), F32),
            scratch((MAXOFF,) + tile, BF16),
            scratch((size, tile_w, width), F32),
            scratch((size, tile_w, width), F32),
            scratch((MAXOFF,) + tile, BF16),
            scratch((MAXOFF,) + tile, BF16),
            scratch(tile, F32),
            scratch((2,) + tile, F32),
            scratch((2, chans, tile_w, local, width), BF16),
            scratch((2, local // grad_per, width), BF16),
            scratch((2, len(SIDES), chans, local // grad_per, width), BF16),
            scratch((2, 2, chans, local, width), BF16),
            scratch(views, BF16),
            scratch((max(group, 2), rows, 9 * channels), BF16),
            scratch((max(group, 2), rows, 9 * channels), BF16),
            dma((count,)),
            dma((count,)),
            dma((9,)),
        ],
        compiler_params=pltpu.CompilerParams(
            collective_id=0, has_side_effects=True, vmem_limit_bytes=60 * 1024 * 1024
        ),
    )(
        offsets,
        features,
        vol_target,
        layer_input,
        w_first.transpose(2, 3, 0, 1),
        w_second.transpose(2, 3, 0, 1),
    )
    if not group:
        summed = lax.all_gather(lax.psum(summed, ("row", "col")), "chan")
        summed = summed.reshape(chans, 2, local, 9 * channels)
    grad_features, first, second = pl.pallas_call(
        write_kernel,
        out_shape=[shape((2,) + tile, BF16)] + [shape((9, channels, channels), F32)] * 2,
        in_specs=[vmem()] * 2,
        out_specs=[vmem()] * 3,
        compiler_params=pltpu.CompilerParams(vmem_limit_bytes=60 * 1024 * 1024),
    )(grad_features, summed)
    first = first.reshape(3, 3, channels, channels).transpose(2, 3, 0, 1)
    second = second.reshape(3, 3, channels, channels).transpose(2, 3, 0, 1)
    return grad_features, first, second


def solution(mesh):
    return jax.shard_map(
        functools.partial(body, dict(mesh.shape)),
        mesh=mesh,
        in_specs=(
            P(None, None, ("groups", "col"), "row"),
            P(None, "chan", ("groups", "col"), "row"),
            P("chan", None, ("groups", "col"), "row"),
            P("row", ("groups", "col")),
            P(),
            P(),
        ),
        out_specs=(
            P(None, "chan", ("groups", "col"), "row"),
            P("groups", None, None, None),
            P("groups", None, None, None),
        ),
        check_vma=False,
    )
```

```python
import functools
import math

import jax
import jax.numpy as jnp
from jax import lax
from jax.experimental import pallas as pl
from jax.experimental.pallas import tpu as pltpu
from jax.sharding import PartitionSpec as P

MAXOFF = 2
REACH = MAXOFF + 1
MESH = pl.DeviceIdType.MESH
SIDES = [(dr, dc) for dr in (-1, 1) for dc in (-1, 0, 1)]
F32 = jnp.float32
BF16 = jnp.bfloat16


def vmem():
    return pl.BlockSpec(memory_space=pltpu.VMEM)


def rolled(value, by):
    by = by % value.shape[-1]
    return value if by == 0 else pltpu.roll(value, by, value.ndim - 1)


def lane_index(shape):
    return lax.broadcasted_iota(jnp.int32, shape, len(shape) - 1)


def either(condition, value, lanes):
    start = jnp.where(condition, 0, lanes.shape[-1])
    return jnp.where(lanes >= start, value, 0.0)


class Links:
    def __init__(self, sizes, send_sem, recv_sem):
        self.sizes = sizes
        self.at = {axis: lax.axis_index(axis) for axis in sizes}
        self.send_sem, self.recv_sem = send_sem, recv_sem
        self.used = 0

    def exists(self, move):
        found = None
        for axis, by in move.items():
            if axis == "chan" or by == 0:
                continue
            there = self.at[axis] + by
            here = jnp.logical_and(there >= 0, there < self.sizes[axis])
            found = here if found is None else jnp.logical_and(found, here)
        return found

    def where(self, move):
        return {
            axis: lax.rem(self.at[axis] + (by + self.sizes[axis]), self.sizes[axis])
            for axis, by in move.items()
        }

    def when(self, move, action):
        found = self.exists(move)
        if found is None:
            action()
        else:
            pl.when(found)(action)

    def back(self, move):
        return {axis: -by for axis, by in move.items()}

    def greet(self, moves, group):
        barrier = pltpu.get_barrier_semaphore()
        count = 0
        for move in moves:
            origin = self.back(move)
            self.when(
                origin,
                lambda origin=origin: pl.semaphore_signal(
                    barrier, inc=1, device_id=self.where(origin), device_id_type=MESH
                ),
            )
            found = self.exists(move)
            count = count + (1 if found is None else found.astype(jnp.int32))
        for by in range(1, group):
            device = self.peer(-by, group)[1]
            pl.semaphore_signal(barrier, inc=1, device_id=device, device_id_type=MESH)
            count = count + 1
        return count

    def greeted(self, count):
        pl.semaphore_wait(pltpu.get_barrier_semaphore(), count)

    def peer(self, by, group):
        cols = self.sizes["col"]
        me = self.at["row"] * cols + self.at["col"]
        rank = lax.rem(me + by + group, group)
        return rank, {"row": lax.div(rank, cols), "col": lax.rem(rank, cols)}

    def copy(self, src, dst, device):
        at = self.used
        self.used += 1
        return pltpu.make_async_remote_copy(
            src_ref=src,
            dst_ref=dst,
            send_sem=self.send_sem.at[at],
            recv_sem=self.recv_sem.at[at],
            device_id=device,
            device_id_type=MESH,
        )

    def send(self, move, src, dst):
        copy = self.copy(src, dst, self.where(move))
        self.when(move, copy.start)
        return move, copy

    def received(self, sent):
        for move, copy in sent:
            self.when(self.back(move), copy.wait_recv)

    def left(self, sent):
        for move, copy in sent:
            self.when(move, copy.wait_send)


def packed_edges(tiles, per):
    count = len(tiles)
    rows = tiles[0].shape[0] // per
    lanes = lane_index((rows, tiles[0].shape[1]))
    packed = jnp.zeros(lanes.shape, F32)
    for q in range(per):
        first = q * 2 * count
        for k, tile in enumerate(tiles):
            piece = tile[q * rows : (q + 1) * rows]
            packed = jnp.where(lanes == first + k, rolled(piece, first + k + 1), packed)
            packed = jnp.where(
                lanes == first + count + k, rolled(piece, first + count + k), packed
            )
    return packed


def spread(blocks, by, per, count):
    return jnp.concatenate(
        [rolled(block, by - q * 2 * count) for block in blocks for q in range(per)], axis=0
    )


def fill_views(views, links, n, tile_of, side_of, edges_of, tile_w, lanes, per, count, first):
    width = lanes.shape[1]
    for dc in (-1, 0, 1):
        before = edges_of(SIDES.index((-1, dc)))
        after = edges_of(SIDES.index((1, dc)))
        slim = lane_index(before[0].shape)
        before = [either(links.exists({"row": -1, "col": dc}), b, slim) for b in before]
        after = [either(links.exists({"row": 1, "col": dc}), b, slim) for b in after]
        for xx in {-1: [0], 0: range(1, tile_w + 1), 1: [tile_w + 1]}[dc]:
            if dc == 0:
                tile, k = tile_of(xx - 1), first + xx - 1
            else:
                tile = either(links.exists({"col": dc}), side_of(0 if dc < 0 else 1), lanes)
                k = first + (tile_w - 1 if dc < 0 else 0)
            left = jnp.where(lanes == 0, spread(before, -k, per, count), rolled(tile, 1))
            right = jnp.where(
                lanes == width - 1,
                spread(after, width - 1 - count - k, per, count),
                rolled(tile, -1),
            )
            views[n, xx, 0] = left.astype(BF16)
            views[n, xx, 1] = tile.astype(BF16)
            views[n, xx, 2] = right.astype(BF16)


EDGE_MOVES = [{"row": -dr, "col": -dc} for dr, dc in SIDES]
SIDE_MOVES = [{"col": 1}, {"col": -1}]


def whole_kernel(
    sizes, group, offset_ref, features_hbm, target_hbm, image_hbm, w1_hbm, w2_hbm,
    grad_out, sum_out,
    grad_ref, sum_ref, features_ref, target_ref, image_ref, w1_ref, w2_ref, far_out, far_in, far_back, far_home,
    image, image_pack, image_edges, image_side, image_views, hidden_s, w1, w2, turned, turned_w,
    window, main_s, spill_s, outgoing, arrived, own, rounded, full, grad_pack, grad_edges,
    grad_side, grad_views, part, parts, send_sem, recv_sem, load_sem,
):
    links = Links(sizes, send_sem, recv_sem)
    images, channels, tile_w, width = image_ref.shape
    local = features_ref.shape[1]
    groups, disp = target_ref.shape[:2]
    size = local // groups
    inv = 1.0 / size
    chans = sizes["chan"]
    chan = links.at["chan"]
    row = links.at["row"]
    direct = group > 0
    forward = [{"row": k} for k in range(1, REACH + 1)]
    backward = [{"row": -k} for k in range(1, REACH + 1)]
    with_chan = [{**move, "chan": c} for move in EDGE_MOVES + SIDE_MOVES for c in range(chans)]
    partners = [{"chan": c} for c in range(1, chans)]
    met = with_chan + partners
    if direct:
        met = [move for move in met if move["chan"]]
    else:
        met = met + forward + backward
    loads = [
        pltpu.make_async_copy(src, dst, load_sem.at[i])
        for i, (src, dst) in enumerate([
            (features_hbm.at[1], features_ref.at[1]),
            (image_hbm, image_ref),
            (w1_hbm, w1_ref),
            (w2_hbm, w2_ref),
            (features_hbm.at[0], features_ref.at[0]),
            (target_hbm, target_ref),
        ])
    ]
    for load in loads:
        load.start()
    expected = links.greet(met, group)
    pending = []
    lanes = lane_index((channels, width))
    small = lane_index((tile_w, width))
    abreast = width // disp

    def packed_far(values, dst, first):
        for i in range(first, first + -(-size // abreast)):
            packed = None
            for r in range(abreast):
                c = (i - first) * abreast + r
                if c < size:
                    value = rolled(values[c], disp + r * disp)
                    packed = value if r == 0 else jnp.where(small >= r * disp, value, packed)
            dst[i] = packed.astype(BF16)

    def unpacked_far(src, first):
        return jnp.stack([
            rolled(src[first + c // abreast].astype(F32), width - disp - (c % abreast) * disp)
            for c in range(size)
        ])

    far = -(-size // abreast)

    def far_of(g):
        return pl.ds(g * far, far)

    loads[0].wait()
    for g in range(groups):
        packed_far(features_ref[1, g * size : (g + 1) * size].astype(F32), far_out, g * far)

    loads[1].wait()
    for n in range(images):
        turned[...] = image_ref[n].astype(F32)
        for x in range(tile_w):
            image[n, x] = turned[:, x, :].astype(BF16)
    count = images * tile_w
    image_per = channels // image_pack.shape[0]
    image_pack[...] = packed_edges(
        [image[n, x].astype(F32) for n in range(images) for x in range(tile_w)], image_per
    ).astype(BF16)
    links.greeted(expected)

    def parts_of(g):
        return pl.ds(g * size, size)

    fetched = {}
    starts = sorted({min(at, groups) for at in (0, 1, 2, groups)})

    def fetch(g, after):
        chosen = pl.ds(g * size, (after - g) * size)
        far_chosen = pl.ds(g * far, (after - g) * far)
        fetched[g] = [
            links.send(move, features_ref.at[1, chosen], window.at[k, chosen])
            for k, move in enumerate(forward[:MAXOFF])
        ]
        fetched[g].append(
            links.send(forward[MAXOFF], far_out.at[far_chosen], far_in.at[far_chosen])
        )
        pending.extend(fetched[g])

    fetch(*starts[:2])
    border = [
        links.send(move, image.at[:, x], image_side.at[side])
        for side, (x, move) in enumerate(zip((tile_w - 1, 0), SIDE_MOVES))
    ]
    border += [
        links.send(move, image_pack, image_edges.at[j]) for j, move in enumerate(EDGE_MOVES)
    ]
    pending += border
    for g, after in zip(starts[1:], starts[2:]):
        fetch(g, after)

    loads[2].wait()
    loads[3].wait()
    first_ch = pl.multiple_of(chan * local, local)
    mine = pl.ds(first_ch, local)
    taps = [(a, b) for a in range(3) for b in range(3)]
    w1[...] = jnp.concatenate([w1_ref[a, b, mine].astype(F32) for a, b in taps], axis=1).astype(BF16)
    flipped = jnp.concatenate([w2_ref[2 - a, 2 - b].astype(F32) for a, b in taps], axis=0)
    turned_w[...] = flipped.T
    w2[...] = turned_w[mine].astype(BF16)

    links.received(border)
    for n in range(images):
        fill_views(
            image_views, links, n,
            lambda x, n=n: image[n, x].astype(F32),
            lambda side, n=n: image_side[side, n].astype(F32),
            lambda j: [image_edges[j].astype(F32)],
            tile_w, lanes, image_per, count, n * tile_w,
        )

    loads[4].wait()
    loads[5].wait()
    offset = jnp.broadcast_to(offset_ref[...], (tile_w, width))
    inside = small * 0 + row
    main_in = [offset == k for k in range(REACH)]
    spill_in = [
        jnp.logical_and(offset + 1 == k, inside >= k) for k in range(1, REACH + 1)
    ]
    returned = []
    for g in range(groups):
        links.received(fetched.get(g, []))
        chosen = parts_of(g)
        main = jnp.where(main_in[0], features_ref[1, chosen].astype(F32), 0.0)
        spill = jnp.zeros_like(main)
        for k in range(REACH):
            got = window[k, chosen].astype(F32) if k < MAXOFF else unpacked_far(far_in, g * far)
            spill = jnp.where(spill_in[k], got, spill)
            if k + 1 < REACH:
                main = jnp.where(main_in[k + 1], got, main)
        main_s[...] = main
        spill_s[...] = spill

        def step(t, state, g=g, chosen=chosen):
            left_grad, total, early = state
            left = features_ref[0, chosen].astype(F32)
            for j in range(8):
                d = t * 8 + j
                keep = small < width - d
                shifted = pltpu.roll(jnp.where(keep, main_s[...], spill_s[...]), d, 2)
                volume = jnp.sum(left * shifted, axis=0) * inv
                weighted = (volume - target_ref[g, d].astype(F32)) * inv
                left_grad = left_grad + weighted * shifted
                back = pltpu.roll(weighted * left, lax.rem(width - d, width), 2)
                early = jnp.where(small == width - d, total, early)
                total = total + back
            return left_grad, total, early

        zero = jnp.zeros((size, tile_w, width), F32)
        left_grad, total, early = lax.fori_loop(0, disp // 8, step, (zero, zero, zero))
        both = small > width - disp
        main_grad = jnp.where(both, early, total)
        spill_grad = jnp.where(both, total - early, 0.0)
        for k in range(1, REACH + 1):
            piece = jnp.where(spill_in[k - 1], spill_grad, 0.0)
            if k < REACH:
                piece = jnp.where(main_in[k], main_grad, piece)
                outgoing[k - 1, chosen] = piece.astype(BF16)
            else:
                packed_far(piece, far_back, g * far)
        returned.append([
            links.send(backward[k], outgoing.at[k, chosen], arrived.at[k, chosen])
            for k in range(MAXOFF)
        ])
        returned[-1].append(
            links.send(backward[MAXOFF], far_back.at[far_of(g)], far_home.at[far_of(g)])
        )
        pending += returned[-1]
        own[chosen] = jnp.where(main_in[0], main_grad, 0.0)
        left_grad = left_grad.astype(BF16)
        grad_ref[0, chosen] = left_grad
        rounded[0, chosen] = left_grad.astype(F32)

    grad_per = local // grad_pack.shape[1]

    def share(n):
        for x in range(tile_w):
            full[n, chan, x] = rounded[n, :, x, :].astype(BF16)
        sent = [links.send(move, full.at[n, chan], full.at[n, chan]) for move in partners]
        for c in range(chans):
            for side, (x, move) in enumerate(zip((tile_w - 1, 0), SIDE_MOVES)):
                sent.append(links.send(
                    {**move, "chan": c}, full.at[n, chan, x], grad_side.at[n, side, chan]
                ))
        grad_pack[n] = packed_edges(
            [rounded[n, :, x, :] for x in range(tile_w)], grad_per
        ).astype(BF16)
        for c in range(chans):
            for j, move in enumerate(EDGE_MOVES):
                sent.append(links.send(
                    {**move, "chan": c}, grad_pack.at[n], grad_edges.at[n, j, chan]
                ))
        return sent

    def joined(pieces):
        return jnp.concatenate([p.astype(F32) for p in pieces], axis=0)

    contract = (((1,), (1,)), ((), ()))

    def gradients(n, first, second):
        fill_views(
            grad_views, links, n,
            lambda x: joined([full[n, c, x] for c in range(chans)]),
            lambda side: joined([grad_side[n, side, c] for c in range(chans)]),
            lambda j: [grad_edges[n, j, c].astype(F32) for c in range(chans)],
            tile_w, lanes, grad_per, tile_w, 0,
        )
        for at in range(tile_w // abreast_rows):
            view = view_of(grad_views, n, at)
            hidden = hidden_s[n, at]
            total = jnp.dot(w2[...], view, preferred_element_type=F32)
            hidden_grad = jnp.where(hidden.astype(F32) > 0, total, 0.0).astype(BF16)
            second += lax.dot_general(hidden, view, contract, preferred_element_type=F32)
            seen = view_of(image_views, n, at)
            first += lax.dot_general(hidden_grad, seen, contract, preferred_element_type=F32)
        return first, second

    def save(src, dst, at):
        copy = pltpu.make_async_copy(src, dst, load_sem.at[at])
        copy.start()
        return copy

    saves = [save(grad_ref.at[0], grad_out.at[0], 6)]
    left_sent = share(0)
    abreast_rows = hidden_s.shape[3] // width

    def view_of(views, n, at):
        rows = range(at * abreast_rows, (at + 1) * abreast_rows)
        return jnp.concatenate(
            [views[n, x : x + 3].reshape(9 * channels, width) for x in rows], axis=1
        )

    for n in range(images):
        for at in range(tile_w // abreast_rows):
            total = jnp.dot(w1[...], view_of(image_views, n, at), preferred_element_type=F32)
            hidden_s[n, at] = jnp.maximum(total, 0.0).astype(BF16)
    for g in range(groups):
        links.received(returned[g])
        chosen = parts_of(g)
        right_grad = own[chosen]
        for k in range(REACH):
            there = inside + (k + 1) < sizes["row"]
            if k < MAXOFF:
                got = arrived[k, chosen].astype(F32)
            else:
                got = unpacked_far(far_home, g * far)
                there = jnp.logical_and(there, small >= width - disp)
            right_grad = right_grad + jnp.where(there, got, 0.0)
        right_grad = right_grad.astype(BF16)
        grad_ref[1, chosen] = right_grad
        rounded[1, chosen] = right_grad.astype(F32)
    saves.append(save(grad_ref.at[1], grad_out.at[1], 7))
    right_sent = share(1)
    pending += left_sent + right_sent
    empty = jnp.zeros((local, 9 * channels), F32)
    links.received(left_sent)
    first, second = gradients(0, empty, empty)
    links.received(right_sent)
    first, second = gradients(1, first, second)
    pixels = images * tile_w * sizes["col"] * width * sizes["row"]
    factor = 1.0 / math.sqrt(pixels)
    first, second = first * factor, second * factor

    if direct:
        rows = 2 * local // group
        half = group // 2
        for j in range(half):
            part[j] = first[j * rows : (j + 1) * rows].astype(BF16)
            part[half + j] = second[j * rows : (j + 1) * rows].astype(BF16)
        scattered, gathered, relayed = [], [], []
        for by in range(1, group):
            rank, device = links.peer(by, group)
            scattered.append(links.copy(part.at[rank], parts.at[by - 1], device))
            scattered[-1].start()
        links.left(pending)
        me = links.peer(0, group)[0]
        total = part[me].astype(F32)
        for by in range(1, group):
            scattered[by - 1].wait_recv()
            total = total + parts[by - 1].astype(F32)
        sum_ref[chan, me] = total.astype(BF16)
        partner = links.where(partners[0])
        held = sum_ref.at[chan, me]
        for by in range(1, group):
            gathered.append(links.copy(held, held, links.peer(by, group)[1]))
            gathered[-1].start()
        relayed.append(links.copy(held, held, partner))
        relayed[-1].start()
        for by in range(1, group):
            gathered[by - 1].wait_recv()
            held = sum_ref.at[chan, links.peer(-by, group)[0]]
            relayed.append(links.copy(held, held, partner))
            relayed[-1].start()
        for copy in relayed:
            copy.wait_recv()
        saves.append(save(sum_ref, sum_out, 8))
        for copy in scattered + gathered + relayed:
            copy.wait_send()
    else:
        sum_ref[:local] = first
        sum_ref[local:] = second
        saves.append(save(sum_ref, sum_out, 8))
        links.left(pending)
    for copy in saves:
        copy.wait()


def write_kernel(grad_ref, sum_ref, out_ref, first_ref, second_ref):
    out_ref[...] = grad_ref[...]
    chans, pieces = sum_ref.shape[:2]
    channels = first_ref.shape[1]
    half = pieces // 2

    def rows(pick):
        return jnp.concatenate(
            [sum_ref[c, j].astype(F32) for c in range(chans) for j in pick], axis=0
        )

    first = rows(range(half))
    second = rows(range(half, pieces)).T
    for t in range(9):
        chosen = slice(t * channels, (t + 1) * channels)
        first_ref[t] = first[:, chosen]
        second_ref[8 - t] = second[chosen]


def body(sizes, layer_input, features, vol_target, offsets, w_first, w_second):
    images, channels, tile_w, width = layer_input.shape
    local = features.shape[1]
    chans = sizes["chan"]
    shape = jax.ShapeDtypeStruct
    dma = pltpu.SemaphoreType.DMA
    scratch = pltpu.VMEM
    size = local // vol_target.shape[0]
    group = sizes["row"] * sizes["col"]
    if chans != 2 or group % 2 or (2 * local) % (8 * group):
        group = 0
    rows = 2 * local // max(group, 2)
    views = (images, tile_w + 2, 3, channels, width)
    tile = (local, tile_w, width)
    pair = 2 if tile_w % 2 == 0 else 1
    image_per = min(width // (2 * images * tile_w), channels // 16)
    grad_per = min(width // (2 * tile_w), local // 8)
    far = vol_target.shape[0] * -(-size // (width // vol_target.shape[1]))
    count = 2 * REACH * vol_target.shape[0] + 2 + len(SIDES)
    count += images * ((chans - 1) + chans * (2 + len(SIDES))) + 3 * group
    if group:
        summed_shape = shape((chans, group, rows, 9 * channels), BF16)
    else:
        summed_shape = shape((2 * local, 9 * channels), F32)
    grad_features, summed = pl.pallas_call(
        functools.partial(whole_kernel, sizes, group),
        out_shape=[shape((2,) + tile, BF16), summed_shape],
        in_specs=[vmem()] + [pl.BlockSpec(memory_space=pl.ANY)] * 5,
        out_specs=[pl.BlockSpec(memory_space=pl.ANY)] * 2,
        scratch_shapes=[
            scratch((2,) + tile, BF16),
            scratch(summed_shape.shape, summed_shape.dtype),
            scratch(features.shape, BF16),
            scratch(vol_target.shape, BF16),
            scratch(layer_input.shape, BF16),
            scratch((3, 3, channels, channels), BF16),
            scratch((3, 3, channels, channels), BF16),
            scratch((far, tile_w, width), BF16),
            scratch((far, tile_w, width), BF16),
            scratch((far, tile_w, width), BF16),
            scratch((far, tile_w, width), BF16),
            scratch((images, tile_w, channels, width), BF16),
            scratch((channels // image_per, width), BF16),
            scratch((len(SIDES), channels // image_per, width), BF16),
            scratch((2, images, channels, width), BF16),
            scratch(views, BF16),
            scratch((images, tile_w // pair, local, pair * width), BF16),
            scratch((local, 9 * channels), BF16),
            scratch((local, 9 * channels), BF16),
            scratch((channels, tile_w, width), F32),
            scratch((channels, 9 * channels), F32),
            scratch((MAXOFF,) + tile, BF16),
            scratch((size, tile_w, width), F32),
            scratch((size, tile_w, width), F32),
            scratch((MAXOFF,) + tile, BF16),
            scratch((MAXOFF,) + tile, BF16),
            scratch(tile, F32),
            scratch((2,) + tile, F32),
            scratch((2, chans, tile_w, local, width), BF16),
            scratch((2, local // grad_per, width), BF16),
            scratch((2, len(SIDES), chans, local // grad_per, width), BF16),
            scratch((2, 2, chans, local, width), BF16),
            scratch(views, BF16),
            scratch((max(group, 2), rows, 9 * channels), BF16),
            scratch((max(group, 2), rows, 9 * channels), BF16),
            dma((count,)),
            dma((count,)),
            dma((9,)),
        ],
        compiler_params=pltpu.CompilerParams(
            collective_id=0, has_side_effects=True, vmem_limit_bytes=60 * 1024 * 1024
        ),
    )(
        offsets,
        features,
        vol_target,
        layer_input,
        w_first.transpose(2, 3, 0, 1),
        w_second.transpose(2, 3, 0, 1),
    )
    if not group:
        summed = lax.all_gather(lax.psum(summed, ("row", "col")), "chan")
        summed = summed.reshape(chans, 2, local, 9 * channels)
    grad_features, first, second = pl.pallas_call(
        write_kernel,
        out_shape=[shape((2,) + tile, BF16)] + [shape((9, channels, channels), F32)] * 2,
        in_specs=[vmem()] * 2,
        out_specs=[vmem()] * 3,
        compiler_params=pltpu.CompilerParams(vmem_limit_bytes=60 * 1024 * 1024),
    )(grad_features, summed)
    first = first.reshape(3, 3, channels, channels).transpose(2, 3, 0, 1)
    second = second.reshape(3, 3, channels, channels).transpose(2, 3, 0, 1)
    return grad_features, first, second


def solution(mesh):
    return jax.shard_map(
        functools.partial(body, dict(mesh.shape)),
        mesh=mesh,
        in_specs=(
            P(None, None, ("groups", "col"), "row"),
            P(None, "chan", ("groups", "col"), "row"),
            P("chan", None, ("groups", "col"), "row"),
            P("row", ("groups", "col")),
            P(),
            P(),
        ),
        out_specs=(
            P(None, "chan", ("groups", "col"), "row"),
            P("groups", None, None, None),
            P("groups", None, None, None),
        ),
        check_vma=False,
    )
```

```python
import functools
import math

import jax
import jax.numpy as jnp
from jax import lax
from jax.experimental import pallas as pl
from jax.experimental.pallas import tpu as pltpu
from jax.sharding import PartitionSpec as P

MAXOFF = 2
REACH = MAXOFF + 1
MESH = pl.DeviceIdType.MESH
SIDES = [(dr, dc) for dr in (-1, 1) for dc in (-1, 0, 1)]
F32 = jnp.float32
BF16 = jnp.bfloat16


def vmem():
    return pl.BlockSpec(memory_space=pltpu.VMEM)


def rolled(value, by):
    by = by % value.shape[-1]
    return value if by == 0 else pltpu.roll(value, by, value.ndim - 1)


def lane_index(shape):
    return lax.broadcasted_iota(jnp.int32, shape, len(shape) - 1)


def either(condition, value, lanes):
    start = jnp.where(condition, 0, lanes.shape[-1])
    return jnp.where(lanes >= start, value, 0.0)


class Links:
    def __init__(self, sizes, send_sem, recv_sem):
        self.sizes = sizes
        self.at = {axis: lax.axis_index(axis) for axis in sizes}
        self.send_sem, self.recv_sem = send_sem, recv_sem
        self.used = 0

    def exists(self, move):
        found = None
        for axis, by in move.items():
            if axis == "chan" or by == 0:
                continue
            there = self.at[axis] + by
            here = jnp.logical_and(there >= 0, there < self.sizes[axis])
            found = here if found is None else jnp.logical_and(found, here)
        return found

    def where(self, move):
        return {
            axis: lax.rem(self.at[axis] + (by + self.sizes[axis]), self.sizes[axis])
            for axis, by in move.items()
        }

    def when(self, move, action):
        found = self.exists(move)
        if found is None:
            action()
        else:
            pl.when(found)(action)

    def back(self, move):
        return {axis: -by for axis, by in move.items()}

    def greet(self, moves, group):
        barrier = pltpu.get_barrier_semaphore()
        count = 0
        for move in moves:
            origin = self.back(move)
            self.when(
                origin,
                lambda origin=origin: pl.semaphore_signal(
                    barrier, inc=1, device_id=self.where(origin), device_id_type=MESH
                ),
            )
            found = self.exists(move)
            count = count + (1 if found is None else found.astype(jnp.int32))
        for by in range(1, group):
            device = self.peer(-by, group)[1]
            pl.semaphore_signal(barrier, inc=1, device_id=device, device_id_type=MESH)
            count = count + 1
        return count

    def greeted(self, count):
        pl.semaphore_wait(pltpu.get_barrier_semaphore(), count)

    def peer(self, by, group):
        cols = self.sizes["col"]
        me = self.at["row"] * cols + self.at["col"]
        rank = lax.rem(me + by + group, group)
        return rank, {"row": lax.div(rank, cols), "col": lax.rem(rank, cols)}

    def copy(self, src, dst, device):
        at = self.used
        self.used += 1
        return pltpu.make_async_remote_copy(
            src_ref=src,
            dst_ref=dst,
            send_sem=self.send_sem.at[at],
            recv_sem=self.recv_sem.at[at],
            device_id=device,
            device_id_type=MESH,
        )

    def send(self, move, src, dst):
        copy = self.copy(src, dst, self.where(move))
        self.when(move, copy.start)
        return move, copy

    def received(self, sent):
        for move, copy in sent:
            self.when(self.back(move), copy.wait_recv)

    def left(self, sent):
        for move, copy in sent:
            self.when(move, copy.wait_send)


def packed_edges(tiles, per):
    count = len(tiles)
    rows = tiles[0].shape[0] // per
    lanes = lane_index((rows, tiles[0].shape[1]))
    packed = jnp.zeros(lanes.shape, F32)
    for q in range(per):
        first = q * 2 * count
        for k, tile in enumerate(tiles):
            piece = tile[q * rows : (q + 1) * rows]
            packed = jnp.where(lanes == first + k, rolled(piece, first + k + 1), packed)
            packed = jnp.where(
                lanes == first + count + k, rolled(piece, first + count + k), packed
            )
    return packed


def spread(blocks, by, per, count):
    return jnp.concatenate(
        [rolled(block, by - q * 2 * count) for block in blocks for q in range(per)], axis=0
    )


def fill_views(views, links, n, tile_of, side_of, edges_of, tile_w, lanes, per, count, first):
    width = lanes.shape[1]
    for dc in (-1, 0, 1):
        before = edges_of(SIDES.index((-1, dc)))
        after = edges_of(SIDES.index((1, dc)))
        slim = lane_index(before[0].shape)
        before = [either(links.exists({"row": -1, "col": dc}), b, slim) for b in before]
        after = [either(links.exists({"row": 1, "col": dc}), b, slim) for b in after]
        for xx in {-1: [0], 0: range(1, tile_w + 1), 1: [tile_w + 1]}[dc]:
            if dc == 0:
                tile, k = tile_of(xx - 1), first + xx - 1
            else:
                tile = either(links.exists({"col": dc}), side_of(0 if dc < 0 else 1), lanes)
                k = first + (tile_w - 1 if dc < 0 else 0)
            left = jnp.where(lanes == 0, spread(before, -k, per, count), rolled(tile, 1))
            right = jnp.where(
                lanes == width - 1,
                spread(after, width - 1 - count - k, per, count),
                rolled(tile, -1),
            )
            views[n, xx, 0] = left.astype(BF16)
            views[n, xx, 1] = tile.astype(BF16)
            views[n, xx, 2] = right.astype(BF16)


EDGE_MOVES = [{"row": -dr, "col": -dc} for dr, dc in SIDES]
SIDE_MOVES = [{"col": 1}, {"col": -1}]


def whole_kernel(
    sizes, group, offset_ref, features_hbm, target_hbm, image_hbm, w1_hbm, w2_hbm,
    grad_out, sum_out,
    grad_ref, sum_ref, features_ref, target_ref, image_ref, w1_ref, w2_ref, far_out, far_in, far_back, far_home,
    image, image_pack, image_edges, image_side, image_views, hidden_s, w1, w2, turned, turned_w,
    window, main_s, spill_s, outgoing, arrived, own, rounded, full, grad_pack, grad_edges,
    grad_side, grad_views, part, parts, send_sem, recv_sem, load_sem,
):
    links = Links(sizes, send_sem, recv_sem)
    images, channels, tile_w, width = image_ref.shape
    local = features_ref.shape[1]
    groups, disp = target_ref.shape[:2]
    size = local // groups
    inv = 1.0 / size
    chans = sizes["chan"]
    chan = links.at["chan"]
    row = links.at["row"]
    direct = group > 0
    forward = [{"row": k} for k in range(1, REACH + 1)]
    backward = [{"row": -k} for k in range(1, REACH + 1)]
    with_chan = [{**move, "chan": c} for move in EDGE_MOVES + SIDE_MOVES for c in range(chans)]
    partners = [{"chan": c} for c in range(1, chans)]
    met = with_chan + partners
    if direct:
        met = [move for move in met if move["chan"]]
    else:
        met = met + forward + backward
    loads = [
        pltpu.make_async_copy(src, dst, load_sem.at[i])
        for i, (src, dst) in enumerate([
            (features_hbm.at[1], features_ref.at[1]),
            (image_hbm, image_ref),
            (w1_hbm, w1_ref),
            (w2_hbm, w2_ref),
            (features_hbm.at[0], features_ref.at[0]),
            (target_hbm, target_ref),
        ])
    ]
    for load in loads:
        load.start()
    expected = links.greet(met, group)
    pending = []
    lanes = lane_index((channels, width))
    small = lane_index((tile_w, width))
    abreast = width // disp

    def packed_far(values, dst, first):
        for i in range(first, first + -(-size // abreast)):
            packed = None
            for r in range(abreast):
                c = (i - first) * abreast + r
                if c < size:
                    value = rolled(values[c], disp + r * disp)
                    packed = value if r == 0 else jnp.where(small >= r * disp, value, packed)
            dst[i] = packed.astype(BF16)

    def unpacked_far(src, first):
        return jnp.stack([
            rolled(src[first + c // abreast].astype(F32), width - disp - (c % abreast) * disp)
            for c in range(size)
        ])

    far = -(-size // abreast)

    def far_of(g):
        return pl.ds(g * far, far)

    loads[0].wait()
    for g in range(groups):
        packed_far(features_ref[1, g * size : (g + 1) * size].astype(F32), far_out, g * far)

    links.greeted(expected)

    def parts_of(g):
        return pl.ds(g * size, size)

    fetched = {}
    starts = sorted({min(at, groups) for at in (0, 1, 2, groups)})

    def fetch(g, after):
        chosen = pl.ds(g * size, (after - g) * size)
        far_chosen = pl.ds(g * far, (after - g) * far)
        fetched[g] = [
            links.send(move, features_ref.at[1, chosen], window.at[k, chosen])
            for k, move in enumerate(forward[:MAXOFF])
        ]
        fetched[g].append(
            links.send(forward[MAXOFF], far_out.at[far_chosen], far_in.at[far_chosen])
        )
        pending.extend(fetched[g])

    fetch(*starts[:2])
    for g, after in zip(starts[1:], starts[2:]):
        fetch(g, after)

    loads[1].wait()
    for n in range(images):
        turned[...] = image_ref[n].astype(F32)
        for x in range(tile_w):
            image[n, x] = turned[:, x, :].astype(BF16)
    count = images * tile_w
    image_per = channels // image_pack.shape[0]
    image_pack[...] = packed_edges(
        [image[n, x].astype(F32) for n in range(images) for x in range(tile_w)], image_per
    ).astype(BF16)
    border = [
        links.send(move, image.at[:, x], image_side.at[side])
        for side, (x, move) in enumerate(zip((tile_w - 1, 0), SIDE_MOVES))
    ]
    border += [
        links.send(move, image_pack, image_edges.at[j]) for j, move in enumerate(EDGE_MOVES)
    ]
    pending += border

    loads[2].wait()
    loads[3].wait()
    first_ch = pl.multiple_of(chan * local, local)
    mine = pl.ds(first_ch, local)
    taps = [(a, b) for a in range(3) for b in range(3)]
    w1[...] = jnp.concatenate([w1_ref[a, b, mine].astype(F32) for a, b in taps], axis=1).astype(BF16)
    flipped = jnp.concatenate([w2_ref[2 - a, 2 - b].astype(F32) for a, b in taps], axis=0)
    turned_w[...] = flipped.T
    w2[...] = turned_w[mine].astype(BF16)

    loads[4].wait()
    loads[5].wait()
    offset = jnp.broadcast_to(offset_ref[...], (tile_w, width))
    inside = small * 0 + row
    main_in = [offset == k for k in range(REACH)]
    spill_in = [
        jnp.logical_and(offset + 1 == k, inside >= k) for k in range(1, REACH + 1)
    ]
    returned = []
    for g in range(groups):
        links.received(fetched.get(g, []))
        chosen = parts_of(g)
        main = jnp.where(main_in[0], features_ref[1, chosen].astype(F32), 0.0)
        spill = jnp.zeros_like(main)
        for k in range(REACH):
            got = window[k, chosen].astype(F32) if k < MAXOFF else unpacked_far(far_in, g * far)
            spill = jnp.where(spill_in[k], got, spill)
            if k + 1 < REACH:
                main = jnp.where(main_in[k + 1], got, main)
        main_s[...] = main
        spill_s[...] = spill

        def step(t, state, g=g, chosen=chosen):
            left_grad, total, early = state
            left = features_ref[0, chosen].astype(F32)
            for j in range(8):
                d = t * 8 + j
                keep = small < width - d
                shifted = pltpu.roll(jnp.where(keep, main_s[...], spill_s[...]), d, 2)
                volume = jnp.sum(left * shifted, axis=0) * inv
                weighted = (volume - target_ref[g, d].astype(F32)) * inv
                left_grad = left_grad + weighted * shifted
                back = pltpu.roll(weighted * left, lax.rem(width - d, width), 2)
                early = jnp.where(small == width - d, total, early)
                total = total + back
            return left_grad, total, early

        zero = jnp.zeros((size, tile_w, width), F32)
        left_grad, total, early = lax.fori_loop(0, disp // 8, step, (zero, zero, zero))
        both = small > width - disp
        main_grad = jnp.where(both, early, total)
        spill_grad = jnp.where(both, total - early, 0.0)
        for k in range(1, REACH + 1):
            piece = jnp.where(spill_in[k - 1], spill_grad, 0.0)
            if k < REACH:
                piece = jnp.where(main_in[k], main_grad, piece)
                outgoing[k - 1, chosen] = piece.astype(BF16)
            else:
                packed_far(piece, far_back, g * far)
        returned.append([
            links.send(backward[k], outgoing.at[k, chosen], arrived.at[k, chosen])
            for k in range(MAXOFF)
        ])
        returned[-1].append(
            links.send(backward[MAXOFF], far_back.at[far_of(g)], far_home.at[far_of(g)])
        )
        pending += returned[-1]
        own[chosen] = jnp.where(main_in[0], main_grad, 0.0)
        left_grad = left_grad.astype(BF16)
        grad_ref[0, chosen] = left_grad
        rounded[0, chosen] = left_grad.astype(F32)

    grad_per = local // grad_pack.shape[1]

    def share(n):
        for x in range(tile_w):
            full[n, chan, x] = rounded[n, :, x, :].astype(BF16)
        sent = [links.send(move, full.at[n, chan], full.at[n, chan]) for move in partners]
        for c in range(chans):
            for side, (x, move) in enumerate(zip((tile_w - 1, 0), SIDE_MOVES)):
                sent.append(links.send(
                    {**move, "chan": c}, full.at[n, chan, x], grad_side.at[n, side, chan]
                ))
        grad_pack[n] = packed_edges(
            [rounded[n, :, x, :] for x in range(tile_w)], grad_per
        ).astype(BF16)
        for c in range(chans):
            for j, move in enumerate(EDGE_MOVES):
                sent.append(links.send(
                    {**move, "chan": c}, grad_pack.at[n], grad_edges.at[n, j, chan]
                ))
        return sent

    def joined(pieces):
        return jnp.concatenate([p.astype(F32) for p in pieces], axis=0)

    contract = (((1,), (1,)), ((), ()))

    def gradients(n, first, second):
        fill_views(
            grad_views, links, n,
            lambda x: joined([full[n, c, x] for c in range(chans)]),
            lambda side: joined([grad_side[n, side, c] for c in range(chans)]),
            lambda j: [grad_edges[n, j, c].astype(F32) for c in range(chans)],
            tile_w, lanes, grad_per, tile_w, 0,
        )
        for at in range(tile_w // abreast_rows):
            view = view_of(grad_views, n, at)
            hidden = hidden_s[n, at]
            total = jnp.dot(w2[...], view, preferred_element_type=F32)
            hidden_grad = jnp.where(hidden.astype(F32) > 0, total, 0.0).astype(BF16)
            second += lax.dot_general(hidden, view, contract, preferred_element_type=F32)
            seen = view_of(image_views, n, at)
            first += lax.dot_general(hidden_grad, seen, contract, preferred_element_type=F32)
        return first, second

    def save(src, dst, at):
        copy = pltpu.make_async_copy(src, dst, load_sem.at[at])
        copy.start()
        return copy

    saves = [save(grad_ref.at[0], grad_out.at[0], 6)]
    left_sent = share(0)
    abreast_rows = hidden_s.shape[3] // width

    def view_of(views, n, at):
        rows = range(at * abreast_rows, (at + 1) * abreast_rows)
        return jnp.concatenate(
            [views[n, x : x + 3].reshape(9 * channels, width) for x in rows], axis=1
        )

    links.received(border)
    for n in range(images):
        fill_views(
            image_views, links, n,
            lambda x, n=n: image[n, x].astype(F32),
            lambda side, n=n: image_side[side, n].astype(F32),
            lambda j: [image_edges[j].astype(F32)],
            tile_w, lanes, image_per, count, n * tile_w,
        )

    def recompute_hidden(n):
        for at in range(tile_w // abreast_rows):
            total = jnp.dot(w1[...], view_of(image_views, n, at), preferred_element_type=F32)
            hidden_s[n, at] = jnp.maximum(total, 0.0).astype(BF16)

    recompute_hidden(0)
    for g in range(groups):
        links.received(returned[g])
        chosen = parts_of(g)
        right_grad = own[chosen]
        for k in range(REACH):
            there = inside + (k + 1) < sizes["row"]
            if k < MAXOFF:
                got = arrived[k, chosen].astype(F32)
            else:
                got = unpacked_far(far_home, g * far)
                there = jnp.logical_and(there, small >= width - disp)
            right_grad = right_grad + jnp.where(there, got, 0.0)
        right_grad = right_grad.astype(BF16)
        grad_ref[1, chosen] = right_grad
        rounded[1, chosen] = right_grad.astype(F32)
    saves.append(save(grad_ref.at[1], grad_out.at[1], 7))
    right_sent = share(1)
    pending += left_sent + right_sent
    empty = jnp.zeros((local, 9 * channels), F32)
    links.received(left_sent)
    first, second = gradients(0, empty, empty)
    recompute_hidden(1)
    links.received(right_sent)
    first, second = gradients(1, first, second)
    pixels = images * tile_w * sizes["col"] * width * sizes["row"]
    factor = 1.0 / math.sqrt(pixels)
    first, second = first * factor, second * factor

    if direct:
        rows = 2 * local // group
        half = group // 2
        for j in range(half):
            part[j] = first[j * rows : (j + 1) * rows].astype(BF16)
            part[half + j] = second[j * rows : (j + 1) * rows].astype(BF16)
        scattered, gathered, relayed = [], [], []
        for by in range(1, group):
            rank, device = links.peer(by, group)
            scattered.append(links.copy(part.at[rank], parts.at[by - 1], device))
            scattered[-1].start()
        links.left(pending)
        me = links.peer(0, group)[0]
        total = part[me].astype(F32)
        for by in range(1, group):
            scattered[by - 1].wait_recv()
            total = total + parts[by - 1].astype(F32)
        sum_ref[chan, me] = total.astype(BF16)
        partner = links.where(partners[0])
        held = sum_ref.at[chan, me]
        for by in range(1, group):
            gathered.append(links.copy(held, held, links.peer(by, group)[1]))
            gathered[-1].start()
        relayed.append(links.copy(held, held, partner))
        relayed[-1].start()
        for by in range(1, group):
            gathered[by - 1].wait_recv()
            held = sum_ref.at[chan, links.peer(-by, group)[0]]
            relayed.append(links.copy(held, held, partner))
            relayed[-1].start()
        for copy in relayed:
            copy.wait_recv()
        saves.append(save(sum_ref, sum_out, 8))
        for copy in scattered + gathered + relayed:
            copy.wait_send()
    else:
        sum_ref[:local] = first
        sum_ref[local:] = second
        saves.append(save(sum_ref, sum_out, 8))
        links.left(pending)
    for copy in saves:
        copy.wait()


def write_kernel(grad_ref, sum_ref, out_ref, first_ref, second_ref):
    out_ref[...] = grad_ref[...]
    chans, pieces = sum_ref.shape[:2]
    channels = first_ref.shape[1]
    half = pieces // 2

    def rows(pick):
        return jnp.concatenate(
            [sum_ref[c, j].astype(F32) for c in range(chans) for j in pick], axis=0
        )

    first = rows(range(half))
    second = rows(range(half, pieces)).T
    for t in range(9):
        chosen = slice(t * channels, (t + 1) * channels)
        first_ref[t] = first[:, chosen]
        second_ref[8 - t] = second[chosen]


def body(sizes, layer_input, features, vol_target, offsets, w_first, w_second):
    images, channels, tile_w, width = layer_input.shape
    local = features.shape[1]
    chans = sizes["chan"]
    shape = jax.ShapeDtypeStruct
    dma = pltpu.SemaphoreType.DMA
    scratch = pltpu.VMEM
    size = local // vol_target.shape[0]
    group = sizes["row"] * sizes["col"]
    if chans != 2 or group % 2 or (2 * local) % (8 * group):
        group = 0
    rows = 2 * local // max(group, 2)
    views = (images, tile_w + 2, 3, channels, width)
    tile = (local, tile_w, width)
    pair = 2 if tile_w % 2 == 0 else 1
    image_per = min(width // (2 * images * tile_w), channels // 16)
    grad_per = min(width // (2 * tile_w), local // 8)
    far = vol_target.shape[0] * -(-size // (width // vol_target.shape[1]))
    count = 2 * REACH * vol_target.shape[0] + 2 + len(SIDES)
    count += images * ((chans - 1) + chans * (2 + len(SIDES))) + 3 * group
    if group:
        summed_shape = shape((chans, group, rows, 9 * channels), BF16)
    else:
        summed_shape = shape((2 * local, 9 * channels), F32)
    grad_features, summed = pl.pallas_call(
        functools.partial(whole_kernel, sizes, group),
        out_shape=[shape((2,) + tile, BF16), summed_shape],
        in_specs=[vmem()] + [pl.BlockSpec(memory_space=pl.ANY)] * 5,
        out_specs=[pl.BlockSpec(memory_space=pl.ANY)] * 2,
        scratch_shapes=[
            scratch((2,) + tile, BF16),
            scratch(summed_shape.shape, summed_shape.dtype),
            scratch(features.shape, BF16),
            scratch(vol_target.shape, BF16),
            scratch(layer_input.shape, BF16),
            scratch((3, 3, channels, channels), BF16),
            scratch((3, 3, channels, channels), BF16),
            scratch((far, tile_w, width), BF16),
            scratch((far, tile_w, width), BF16),
            scratch((far, tile_w, width), BF16),
            scratch((far, tile_w, width), BF16),
            scratch((images, tile_w, channels, width), BF16),
            scratch((channels // image_per, width), BF16),
            scratch((len(SIDES), channels // image_per, width), BF16),
            scratch((2, images, channels, width), BF16),
            scratch(views, BF16),
            scratch((images, tile_w // pair, local, pair * width), BF16),
            scratch((local, 9 * channels), BF16),
            scratch((local, 9 * channels), BF16),
            scratch((channels, tile_w, width), F32),
            scratch((channels, 9 * channels), F32),
            scratch((MAXOFF,) + tile, BF16),
            scratch((size, tile_w, width), F32),
            scratch((size, tile_w, width), F32),
            scratch((MAXOFF,) + tile, BF16),
            scratch((MAXOFF,) + tile, BF16),
            scratch(tile, F32),
            scratch((2,) + tile, F32),
            scratch((2, chans, tile_w, local, width), BF16),
            scratch((2, local // grad_per, width), BF16),
            scratch((2, len(SIDES), chans, local // grad_per, width), BF16),
            scratch((2, 2, chans, local, width), BF16),
            scratch(views, BF16),
            scratch((max(group, 2), rows, 9 * channels), BF16),
            scratch((max(group, 2), rows, 9 * channels), BF16),
            dma((count,)),
            dma((count,)),
            dma((9,)),
        ],
        compiler_params=pltpu.CompilerParams(
            collective_id=0, has_side_effects=True, vmem_limit_bytes=60 * 1024 * 1024
        ),
    )(
        offsets,
        features,
        vol_target,
        layer_input,
        w_first.transpose(2, 3, 0, 1),
        w_second.transpose(2, 3, 0, 1),
    )
    if not group:
        summed = lax.all_gather(lax.psum(summed, ("row", "col")), "chan")
        summed = summed.reshape(chans, 2, local, 9 * channels)
    grad_features, first, second = pl.pallas_call(
        write_kernel,
        out_shape=[shape((2,) + tile, BF16)] + [shape((9, channels, channels), F32)] * 2,
        in_specs=[vmem()] * 2,
        out_specs=[vmem()] * 3,
        compiler_params=pltpu.CompilerParams(vmem_limit_bytes=60 * 1024 * 1024),
    )(grad_features, summed)
    first = first.reshape(3, 3, channels, channels).transpose(2, 3, 0, 1)
    second = second.reshape(3, 3, channels, channels).transpose(2, 3, 0, 1)
    return grad_features, first, second


def solution(mesh):
    return jax.shard_map(
        functools.partial(body, dict(mesh.shape)),
        mesh=mesh,
        in_specs=(
            P(None, None, ("groups", "col"), "row"),
            P(None, "chan", ("groups", "col"), "row"),
            P("chan", None, ("groups", "col"), "row"),
            P("row", ("groups", "col")),
            P(),
            P(),
        ),
        out_specs=(
            P(None, "chan", ("groups", "col"), "row"),
            P("groups", None, None, None),
            P("groups", None, None, None),
        ),
        check_vma=False,
    )
```

```python
import functools
import math

import jax
import jax.numpy as jnp
from jax import lax
from jax.experimental import pallas as pl
from jax.experimental.pallas import tpu as pltpu
from jax.sharding import PartitionSpec as P

MAXOFF = 2
REACH = MAXOFF + 1
MESH = pl.DeviceIdType.MESH
SIDES = [(dr, dc) for dr in (-1, 1) for dc in (-1, 0, 1)]
F32 = jnp.float32
BF16 = jnp.bfloat16


def vmem():
    return pl.BlockSpec(memory_space=pltpu.VMEM)


def rolled(value, by):
    by = by % value.shape[-1]
    return value if by == 0 else pltpu.roll(value, by, value.ndim - 1)


def lane_index(shape):
    return lax.broadcasted_iota(jnp.int32, shape, len(shape) - 1)


def either(condition, value, lanes):
    start = jnp.where(condition, 0, lanes.shape[-1])
    return jnp.where(lanes >= start, value, 0.0)


class Links:
    def __init__(self, sizes, send_sem, recv_sem):
        self.sizes = sizes
        self.at = {axis: lax.axis_index(axis) for axis in sizes}
        self.send_sem, self.recv_sem = send_sem, recv_sem
        self.used = 0

    def exists(self, move):
        found = None
        for axis, by in move.items():
            if axis == "chan" or by == 0:
                continue
            there = self.at[axis] + by
            here = jnp.logical_and(there >= 0, there < self.sizes[axis])
            found = here if found is None else jnp.logical_and(found, here)
        return found

    def where(self, move):
        return {
            axis: lax.rem(self.at[axis] + (by + self.sizes[axis]), self.sizes[axis])
            for axis, by in move.items()
        }

    def when(self, move, action):
        found = self.exists(move)
        if found is None:
            action()
        else:
            pl.when(found)(action)

    def back(self, move):
        return {axis: -by for axis, by in move.items()}

    def greet(self, moves, group):
        barrier = pltpu.get_barrier_semaphore()
        count = 0
        for move in moves:
            origin = self.back(move)
            self.when(
                origin,
                lambda origin=origin: pl.semaphore_signal(
                    barrier, inc=1, device_id=self.where(origin), device_id_type=MESH
                ),
            )
            found = self.exists(move)
            count = count + (1 if found is None else found.astype(jnp.int32))
        for by in range(1, group):
            device = self.peer(-by, group)[1]
            pl.semaphore_signal(barrier, inc=1, device_id=device, device_id_type=MESH)
            count = count + 1
        return count

    def greeted(self, count):
        pl.semaphore_wait(pltpu.get_barrier_semaphore(), count)

    def peer(self, by, group):
        cols = self.sizes["col"]
        me = self.at["row"] * cols + self.at["col"]
        rank = lax.rem(me + by + group, group)
        return rank, {"row": lax.div(rank, cols), "col": lax.rem(rank, cols)}

    def copy(self, src, dst, device):
        at = self.used
        self.used += 1
        return pltpu.make_async_remote_copy(
            src_ref=src,
            dst_ref=dst,
            send_sem=self.send_sem.at[at],
            recv_sem=self.recv_sem.at[at],
            device_id=device,
            device_id_type=MESH,
        )

    def send(self, move, src, dst):
        copy = self.copy(src, dst, self.where(move))
        self.when(move, copy.start)
        return move, copy

    def received(self, sent):
        for move, copy in sent:
            self.when(self.back(move), copy.wait_recv)

    def left(self, sent):
        for move, copy in sent:
            self.when(move, copy.wait_send)


def packed_edges(tiles, per):
    count = len(tiles)
    rows = tiles[0].shape[0] // per
    lanes = lane_index((rows, tiles[0].shape[1]))
    packed = jnp.zeros(lanes.shape, F32)
    for q in range(per):
        first = q * 2 * count
        for k, tile in enumerate(tiles):
            piece = tile[q * rows : (q + 1) * rows]
            packed = jnp.where(lanes == first + k, rolled(piece, first + k + 1), packed)
            packed = jnp.where(
                lanes == first + count + k, rolled(piece, first + count + k), packed
            )
    return packed


def spread(blocks, by, per, count):
    return jnp.concatenate(
        [rolled(block, by - q * 2 * count) for block in blocks for q in range(per)], axis=0
    )


def fill_views(views, links, n, tile_of, side_of, edges_of, tile_w, lanes, per, count, first):
    width = lanes.shape[1]
    for dc in (-1, 0, 1):
        before = edges_of(SIDES.index((-1, dc)))
        after = edges_of(SIDES.index((1, dc)))
        slim = lane_index(before[0].shape)
        before = [either(links.exists({"row": -1, "col": dc}), b, slim) for b in before]
        after = [either(links.exists({"row": 1, "col": dc}), b, slim) for b in after]
        for xx in {-1: [0], 0: range(1, tile_w + 1), 1: [tile_w + 1]}[dc]:
            if dc == 0:
                tile, k = tile_of(xx - 1), first + xx - 1
            else:
                tile = either(links.exists({"col": dc}), side_of(0 if dc < 0 else 1), lanes)
                k = first + (tile_w - 1 if dc < 0 else 0)
            left = jnp.where(lanes == 0, spread(before, -k, per, count), rolled(tile, 1))
            right = jnp.where(
                lanes == width - 1,
                spread(after, width - 1 - count - k, per, count),
                rolled(tile, -1),
            )
            views[n, xx, 0] = left.astype(BF16)
            views[n, xx, 1] = tile.astype(BF16)
            views[n, xx, 2] = right.astype(BF16)


EDGE_MOVES = [{"row": -dr, "col": -dc} for dr, dc in SIDES]
SIDE_MOVES = [{"col": 1}, {"col": -1}]


def whole_kernel(
    sizes, group, offset_ref, features_hbm, target_hbm, image_hbm, w1_hbm, w2_hbm,
    grad_out, sum_out,
    grad_ref, sum_ref, features_ref, target_ref, image_ref, w1_ref, w2_ref, far_out, far_in, far_back, far_home,
    image, image_pack, image_edges, image_side, image_views, hidden_s, w1, w2, turned, turned_w,
    window, main_s, spill_s, outgoing, arrived, own, rounded, full, grad_pack, grad_edges,
    grad_side, grad_views, part, parts, send_sem, recv_sem, load_sem,
):
    links = Links(sizes, send_sem, recv_sem)
    images, channels, tile_w, width = image_ref.shape
    local = features_ref.shape[1]
    groups, disp = target_ref.shape[:2]
    size = local // groups
    inv = 1.0 / size
    chans = sizes["chan"]
    chan = links.at["chan"]
    row = links.at["row"]
    direct = group > 0
    forward = [{"row": k} for k in range(1, REACH + 1)]
    backward = [{"row": -k} for k in range(1, REACH + 1)]
    with_chan = [{**move, "chan": c} for move in EDGE_MOVES + SIDE_MOVES for c in range(chans)]
    partners = [{"chan": c} for c in range(1, chans)]
    met = with_chan + partners
    if direct:
        met = [move for move in met if move["chan"]]
    else:
        met = met + forward + backward
    loads = [
        pltpu.make_async_copy(src, dst, load_sem.at[i])
        for i, (src, dst) in enumerate([
            (features_hbm.at[1], features_ref.at[1]),
            (image_hbm, image_ref),
            (w1_hbm, w1_ref),
            (w2_hbm, w2_ref),
            (features_hbm.at[0], features_ref.at[0]),
            (target_hbm, target_ref),
        ])
    ]
    for load in loads:
        load.start()
    expected = links.greet(met, group)
    pending = []
    lanes = lane_index((channels, width))
    small = lane_index((tile_w, width))
    abreast = width // disp

    def packed_far(values, dst, first):
        for i in range(first, first + -(-size // abreast)):
            packed = None
            for r in range(abreast):
                c = (i - first) * abreast + r
                if c < size:
                    value = rolled(values[c], disp + r * disp)
                    packed = value if r == 0 else jnp.where(small >= r * disp, value, packed)
            dst[i] = packed.astype(BF16)

    def unpacked_far(src, first):
        return jnp.stack([
            rolled(src[first + c // abreast].astype(F32), width - disp - (c % abreast) * disp)
            for c in range(size)
        ])

    far = -(-size // abreast)

    def far_of(g):
        return pl.ds(g * far, far)


    links.greeted(expected)

    def parts_of(g):
        return pl.ds(g * size, size)

    fetched = {}
    starts = sorted({min(at, groups) for at in (0, 1, 2, groups)})

    def fetch(g, after):
        chosen = pl.ds(g * size, (after - g) * size)
        fetched[g] = [
            links.send(move, features_hbm.at[1, chosen], window.at[k, chosen])
            for k, move in enumerate(forward[:MAXOFF])
        ]

    def fetch_far(g, after):
        far_chosen = pl.ds(g * far, (after - g) * far)
        fetched[g].append(
            links.send(forward[MAXOFF], far_out.at[far_chosen], far_in.at[far_chosen])
        )
        pending.extend(fetched[g])

    for g, after in zip(starts, starts[1:]):
        fetch(g, after)
    loads[0].wait()
    for g in range(groups):
        packed_far(features_ref[1, g * size : (g + 1) * size].astype(F32), far_out, g * far)
    for g, after in zip(starts, starts[1:]):
        fetch_far(g, after)

    loads[1].wait()
    for n in range(images):
        turned[...] = image_ref[n].astype(F32)
        for x in range(tile_w):
            image[n, x] = turned[:, x, :].astype(BF16)
    count = images * tile_w
    image_per = channels // image_pack.shape[0]
    image_pack[...] = packed_edges(
        [image[n, x].astype(F32) for n in range(images) for x in range(tile_w)], image_per
    ).astype(BF16)
    border = [
        links.send(move, image.at[:, x], image_side.at[side])
        for side, (x, move) in enumerate(zip((tile_w - 1, 0), SIDE_MOVES))
    ]
    border += [
        links.send(move, image_pack, image_edges.at[j]) for j, move in enumerate(EDGE_MOVES)
    ]
    pending += border

    loads[2].wait()
    loads[3].wait()
    first_ch = pl.multiple_of(chan * local, local)
    mine = pl.ds(first_ch, local)
    taps = [(a, b) for a in range(3) for b in range(3)]
    w1[...] = jnp.concatenate([w1_ref[a, b, mine].astype(F32) for a, b in taps], axis=1).astype(BF16)
    flipped = jnp.concatenate([w2_ref[2 - a, 2 - b].astype(F32) for a, b in taps], axis=0)
    turned_w[...] = flipped.T
    w2[...] = turned_w[mine].astype(BF16)

    loads[4].wait()
    loads[5].wait()
    offset = jnp.broadcast_to(offset_ref[...], (tile_w, width))
    inside = small * 0 + row
    main_in = [offset == k for k in range(REACH)]
    spill_in = [
        jnp.logical_and(offset + 1 == k, inside >= k) for k in range(1, REACH + 1)
    ]
    returned = []
    for g in range(groups):
        links.received(fetched.get(g, []))
        chosen = parts_of(g)
        main = jnp.where(main_in[0], features_ref[1, chosen].astype(F32), 0.0)
        spill = jnp.zeros_like(main)
        for k in range(REACH):
            got = window[k, chosen].astype(F32) if k < MAXOFF else unpacked_far(far_in, g * far)
            spill = jnp.where(spill_in[k], got, spill)
            if k + 1 < REACH:
                main = jnp.where(main_in[k + 1], got, main)
        main_s[...] = main
        spill_s[...] = spill

        def step(t, state, g=g, chosen=chosen):
            left_grad, total, early = state
            left = features_ref[0, chosen].astype(F32)
            for j in range(8):
                d = t * 8 + j
                keep = small < width - d
                shifted = pltpu.roll(jnp.where(keep, main_s[...], spill_s[...]), d, 2)
                volume = jnp.sum(left * shifted, axis=0) * inv
                weighted = (volume - target_ref[g, d].astype(F32)) * inv
                left_grad = left_grad + weighted * shifted
                back = pltpu.roll(weighted * left, lax.rem(width - d, width), 2)
                early = jnp.where(small == width - d, total, early)
                total = total + back
            return left_grad, total, early

        zero = jnp.zeros((size, tile_w, width), F32)
        left_grad, total, early = lax.fori_loop(0, disp // 8, step, (zero, zero, zero))
        both = small > width - disp
        main_grad = jnp.where(both, early, total)
        spill_grad = jnp.where(both, total - early, 0.0)
        for k in range(1, REACH + 1):
            piece = jnp.where(spill_in[k - 1], spill_grad, 0.0)
            if k < REACH:
                piece = jnp.where(main_in[k], main_grad, piece)
                outgoing[k - 1, chosen] = piece.astype(BF16)
            else:
                packed_far(piece, far_back, g * far)
        returned.append([
            links.send(backward[k], outgoing.at[k, chosen], arrived.at[k, chosen])
            for k in range(MAXOFF)
        ])
        returned[-1].append(
            links.send(backward[MAXOFF], far_back.at[far_of(g)], far_home.at[far_of(g)])
        )
        pending += returned[-1]
        own[chosen] = jnp.where(main_in[0], main_grad, 0.0)
        left_grad = left_grad.astype(BF16)
        grad_ref[0, chosen] = left_grad
        rounded[0, chosen] = left_grad.astype(F32)

    grad_per = local // grad_pack.shape[1]

    def share(n):
        for x in range(tile_w):
            full[n, chan, x] = rounded[n, :, x, :].astype(BF16)
        sent = [links.send(move, full.at[n, chan], full.at[n, chan]) for move in partners]
        for c in range(chans):
            for side, (x, move) in enumerate(zip((tile_w - 1, 0), SIDE_MOVES)):
                sent.append(links.send(
                    {**move, "chan": c}, full.at[n, chan, x], grad_side.at[n, side, chan]
                ))
        grad_pack[n] = packed_edges(
            [rounded[n, :, x, :] for x in range(tile_w)], grad_per
        ).astype(BF16)
        for c in range(chans):
            for j, move in enumerate(EDGE_MOVES):
                sent.append(links.send(
                    {**move, "chan": c}, grad_pack.at[n], grad_edges.at[n, j, chan]
                ))
        return sent

    def joined(pieces):
        return jnp.concatenate([p.astype(F32) for p in pieces], axis=0)

    contract = (((1,), (1,)), ((), ()))

    def gradients(n, first, second):
        fill_views(
            grad_views, links, n,
            lambda x: joined([full[n, c, x] for c in range(chans)]),
            lambda side: joined([grad_side[n, side, c] for c in range(chans)]),
            lambda j: [grad_edges[n, j, c].astype(F32) for c in range(chans)],
            tile_w, lanes, grad_per, tile_w, 0,
        )
        for at in range(tile_w // abreast_rows):
            view = view_of(grad_views, n, at)
            hidden = hidden_s[n, at]
            total = jnp.dot(w2[...], view, preferred_element_type=F32)
            hidden_grad = jnp.where(hidden.astype(F32) > 0, total, 0.0).astype(BF16)
            second += lax.dot_general(hidden, view, contract, preferred_element_type=F32)
            seen = view_of(image_views, n, at)
            first += lax.dot_general(hidden_grad, seen, contract, preferred_element_type=F32)
        return first, second

    def save(src, dst, at):
        copy = pltpu.make_async_copy(src, dst, load_sem.at[at])
        copy.start()
        return copy

    saves = [save(grad_ref.at[0], grad_out.at[0], 6)]
    left_sent = share(0)
    abreast_rows = hidden_s.shape[3] // width

    def view_of(views, n, at):
        rows = range(at * abreast_rows, (at + 1) * abreast_rows)
        return jnp.concatenate(
            [views[n, x : x + 3].reshape(9 * channels, width) for x in rows], axis=1
        )

    links.received(border)
    for n in range(images):
        fill_views(
            image_views, links, n,
            lambda x, n=n: image[n, x].astype(F32),
            lambda side, n=n: image_side[side, n].astype(F32),
            lambda j: [image_edges[j].astype(F32)],
            tile_w, lanes, image_per, count, n * tile_w,
        )

    def recompute_hidden(n):
        for at in range(tile_w // abreast_rows):
            total = jnp.dot(w1[...], view_of(image_views, n, at), preferred_element_type=F32)
            hidden_s[n, at] = jnp.maximum(total, 0.0).astype(BF16)

    recompute_hidden(0)
    for g in range(groups):
        links.received(returned[g])
        chosen = parts_of(g)
        right_grad = own[chosen]
        for k in range(REACH):
            there = inside + (k + 1) < sizes["row"]
            if k < MAXOFF:
                got = arrived[k, chosen].astype(F32)
            else:
                got = unpacked_far(far_home, g * far)
                there = jnp.logical_and(there, small >= width - disp)
            right_grad = right_grad + jnp.where(there, got, 0.0)
        right_grad = right_grad.astype(BF16)
        grad_ref[1, chosen] = right_grad
        rounded[1, chosen] = right_grad.astype(F32)
    saves.append(save(grad_ref.at[1], grad_out.at[1], 7))
    right_sent = share(1)
    pending += left_sent + right_sent
    empty = jnp.zeros((local, 9 * channels), F32)
    links.received(left_sent)
    first, second = gradients(0, empty, empty)
    recompute_hidden(1)
    links.received(right_sent)
    first, second = gradients(1, first, second)
    pixels = images * tile_w * sizes["col"] * width * sizes["row"]
    factor = 1.0 / math.sqrt(pixels)
    first, second = first * factor, second * factor

    if direct:
        rows = 2 * local // group
        half = group // 2
        for j in range(half):
            part[j] = first[j * rows : (j + 1) * rows].astype(BF16)
            part[half + j] = second[j * rows : (j + 1) * rows].astype(BF16)
        scattered, gathered, relayed = [], [], []
        for by in range(1, group):
            rank, device = links.peer(by, group)
            scattered.append(links.copy(part.at[rank], parts.at[by - 1], device))
            scattered[-1].start()
        links.left(pending)
        me = links.peer(0, group)[0]
        total = part[me].astype(F32)
        for by in range(1, group):
            scattered[by - 1].wait_recv()
            total = total + parts[by - 1].astype(F32)
        sum_ref[chan, me] = total.astype(BF16)
        partner = links.where(partners[0])
        held = sum_ref.at[chan, me]
        for by in range(1, group):
            gathered.append(links.copy(held, held, links.peer(by, group)[1]))
            gathered[-1].start()
        relayed.append(links.copy(held, held, partner))
        relayed[-1].start()
        for by in range(1, group):
            gathered[by - 1].wait_recv()
            held = sum_ref.at[chan, links.peer(-by, group)[0]]
            relayed.append(links.copy(held, held, partner))
            relayed[-1].start()
        for copy in relayed:
            copy.wait_recv()
        saves.append(save(sum_ref, sum_out, 8))
        for copy in scattered + gathered + relayed:
            copy.wait_send()
    else:
        sum_ref[:local] = first
        sum_ref[local:] = second
        saves.append(save(sum_ref, sum_out, 8))
        links.left(pending)
    for copy in saves:
        copy.wait()


def write_kernel(grad_ref, sum_ref, out_ref, first_ref, second_ref):
    out_ref[...] = grad_ref[...]
    chans, pieces = sum_ref.shape[:2]
    channels = first_ref.shape[1]
    half = pieces // 2

    def rows(pick):
        return jnp.concatenate(
            [sum_ref[c, j].astype(F32) for c in range(chans) for j in pick], axis=0
        )

    first = rows(range(half))
    second = rows(range(half, pieces)).T
    for t in range(9):
        chosen = slice(t * channels, (t + 1) * channels)
        first_ref[t] = first[:, chosen]
        second_ref[8 - t] = second[chosen]


def body(sizes, layer_input, features, vol_target, offsets, w_first, w_second):
    images, channels, tile_w, width = layer_input.shape
    local = features.shape[1]
    chans = sizes["chan"]
    shape = jax.ShapeDtypeStruct
    dma = pltpu.SemaphoreType.DMA
    scratch = pltpu.VMEM
    size = local // vol_target.shape[0]
    group = sizes["row"] * sizes["col"]
    if chans != 2 or group % 2 or (2 * local) % (8 * group):
        group = 0
    rows = 2 * local // max(group, 2)
    views = (images, tile_w + 2, 3, channels, width)
    tile = (local, tile_w, width)
    pair = 2 if tile_w % 2 == 0 else 1
    image_per = min(width // (2 * images * tile_w), channels // 16)
    grad_per = min(width // (2 * tile_w), local // 8)
    far = vol_target.shape[0] * -(-size // (width // vol_target.shape[1]))
    count = 2 * REACH * vol_target.shape[0] + 2 + len(SIDES)
    count += images * ((chans - 1) + chans * (2 + len(SIDES))) + 3 * group
    if group:
        summed_shape = shape((chans, group, rows, 9 * channels), BF16)
    else:
        summed_shape = shape((2 * local, 9 * channels), F32)
    grad_features, summed = pl.pallas_call(
        functools.partial(whole_kernel, sizes, group),
        out_shape=[shape((2,) + tile, BF16), summed_shape],
        in_specs=[vmem()] + [pl.BlockSpec(memory_space=pl.ANY)] * 5,
        out_specs=[pl.BlockSpec(memory_space=pl.ANY)] * 2,
        scratch_shapes=[
            scratch((2,) + tile, BF16),
            scratch(summed_shape.shape, summed_shape.dtype),
            scratch(features.shape, BF16),
            scratch(vol_target.shape, BF16),
            scratch(layer_input.shape, BF16),
            scratch((3, 3, channels, channels), BF16),
            scratch((3, 3, channels, channels), BF16),
            scratch((far, tile_w, width), BF16),
            scratch((far, tile_w, width), BF16),
            scratch((far, tile_w, width), BF16),
            scratch((far, tile_w, width), BF16),
            scratch((images, tile_w, channels, width), BF16),
            scratch((channels // image_per, width), BF16),
            scratch((len(SIDES), channels // image_per, width), BF16),
            scratch((2, images, channels, width), BF16),
            scratch(views, BF16),
            scratch((images, tile_w // pair, local, pair * width), BF16),
            scratch((local, 9 * channels), BF16),
            scratch((local, 9 * channels), BF16),
            scratch((channels, tile_w, width), F32),
            scratch((channels, 9 * channels), F32),
            scratch((MAXOFF,) + tile, BF16),
            scratch((size, tile_w, width), F32),
            scratch((size, tile_w, width), F32),
            scratch((MAXOFF,) + tile, BF16),
            scratch((MAXOFF,) + tile, BF16),
            scratch(tile, F32),
            scratch((2,) + tile, F32),
            scratch((2, chans, tile_w, local, width), BF16),
            scratch((2, local // grad_per, width), BF16),
            scratch((2, len(SIDES), chans, local // grad_per, width), BF16),
            scratch((2, 2, chans, local, width), BF16),
            scratch(views, BF16),
            scratch((max(group, 2), rows, 9 * channels), BF16),
            scratch((max(group, 2), rows, 9 * channels), BF16),
            dma((count,)),
            dma((count,)),
            dma((9,)),
        ],
        compiler_params=pltpu.CompilerParams(
            collective_id=0, has_side_effects=True, vmem_limit_bytes=60 * 1024 * 1024
        ),
    )(
        offsets,
        features,
        vol_target,
        layer_input,
        w_first.transpose(2, 3, 0, 1),
        w_second.transpose(2, 3, 0, 1),
    )
    if not group:
        summed = lax.all_gather(lax.psum(summed, ("row", "col")), "chan")
        summed = summed.reshape(chans, 2, local, 9 * channels)
    grad_features, first, second = pl.pallas_call(
        write_kernel,
        out_shape=[shape((2,) + tile, BF16)] + [shape((9, channels, channels), F32)] * 2,
        in_specs=[vmem()] * 2,
        out_specs=[vmem()] * 3,
        compiler_params=pltpu.CompilerParams(vmem_limit_bytes=60 * 1024 * 1024),
    )(grad_features, summed)
    first = first.reshape(3, 3, channels, channels).transpose(2, 3, 0, 1)
    second = second.reshape(3, 3, channels, channels).transpose(2, 3, 0, 1)
    return grad_features, first, second


def solution(mesh):
    return jax.shard_map(
        functools.partial(body, dict(mesh.shape)),
        mesh=mesh,
        in_specs=(
            P(None, None, ("groups", "col"), "row"),
            P(None, "chan", ("groups", "col"), "row"),
            P("chan", None, ("groups", "col"), "row"),
            P("row", ("groups", "col")),
            P(),
            P(),
        ),
        out_specs=(
            P(None, "chan", ("groups", "col"), "row"),
            P("groups", None, None, None),
            P("groups", None, None, None),
        ),
        check_vma=False,
    )
```
